128 devices in a mesh: dp: 4 (over z), expert: 32 (over x, y, core).
Axes of the slice: x: 4, y: 4, z: 4, core: 2. Of those that a mesh axis runs over, the one named last changes fastest.
Arguments:
- block_input: bfloat16 [32, 1024, 1024], P('expert', 'dp'), may hold values from -6 to 6
- attn_norm_gain: float32 [1024], replicated, may hold values from 0.1 to 1.9
- query_proj: bfloat16 [1024, 1024], replicated, may hold values from -0.1875 to 0.1875
- key_proj: bfloat16 [1024, 512], replicated, may hold values from -0.1875 to 0.1875
- value_proj: bfloat16 [1024, 512], replicated, may hold values from -0.1875 to 0.1875
- query_gain: float32 [64], replicated, may hold values from 0.1 to 1.9
- key_gain: float32 [64], replicated, may hold values from 0.1 to 1.9
- output_proj: bfloat16 [1024, 1024], replicated, may hold values from -1 to 1
- ffn_norm_gain: float32 [1024], replicated, may hold values from 0.1 to 1.9
- router_proj: bfloat16 [1024, 32], replicated, may hold values from -0.09375 to 0.09375
- expert_routes: int32 [32, 1024, 8], P('expert', 'dp'), may hold values from 0 to 31, all different within a row; in each aligned block of 256 rows (0 to 255, 256 to 511, ..., all dimensions but the last counted through in order) at most 80 rows name the same one
- document_ids: int32 [32, 1024], P('expert'), may hold values from 0 to 2, as said below
- expert_gate: bfloat16 [32, 1024, 512], P('expert'), may hold values from -0.1875 to 0.1875
- expert_up: bfloat16 [32, 1024, 512], P('expert'), may hold values from -0.1875 to 0.1875
- expert_down: bfloat16 [32, 512, 1024], P('expert'), may hold values from -1 to 1
- cotangent: bfloat16 [32, 1024, 1024], P('expert', 'dp'), may hold values from -6 to 6
Outputs:
- block_output: bfloat16 [32, 1024, 1024], P('expert', 'dp')
- input_grad: float32 [32, 1024, 1024], P('expert', 'dp')
- attn_gain_grad: float32 [1024], replicated
- query_grad: float32 [1024, 1024], replicated
- key_grad: float32 [1024, 512], replicated
- value_grad: float32 [1024, 512], replicated
- query_gain_grad: float32 [64], replicated
- key_gain_grad: float32 [64], replicated
- output_grad: float32 [1024, 1024], replicated
- ffn_gain_grad: float32 [1024], replicated
- router_grad: float32 [1024, 32], replicated
- gate_grad: float32 [32, 1024, 512], P('expert', 'dp')
- up_grad: float32 [32, 1024, 512], P('expert', 'dp')
- down_grad: float32 [32, 512, 1024], P('expert', None, 'dp')
The draws below stay inside these ranges and needn't reach their ends.
Inputs may be any that keep to these rules, and one draw needn't show every extreme that they name: `expert_routes`: each row names 8 different experts; among the 256 tokens of one device no expert is chosen more than 80 times. `document_ids`: never falling along a sequence; document 1 begins within the first 256 tokens and ends within the last 256 tokens.
All inputs are finite; a program needn't handle non-finite values.
Results may differ from the reference program's by a relative error of at most 0.022.
Values may be sent and summed in bfloat16 or wider, within the bound.
No kernel may reach another device: no remote copies, remote signals or barrier semaphores. Data moves between devices by JAX's collectives and lax.ppermute only.
A program may use at most 192 MiB of HBM per device.

```python
import math
import jax
import jax.numpy as jnp
import numpy as np
from jax import lax

D = 1024
HEADS = 16
KV_HEADS = 8
HEAD = 64
FF = 512
EXPERTS = 32
TOPK = 8
TOK_DEV = 256
SEQS = 32
LEN = 1024
CAP = 80
N_DP = 4


def draw_document_ids(key, part):
    key = jax.random.fold_in(key, 7)
    first_key, second_key = jax.random.split(key)
    first_cut = jax.random.randint(first_key, (SEQS, 1), 1, LEN // 4, dtype=jnp.int32)
    second_cut = jax.random.randint(second_key, (SEQS, 1), LEN - LEN // 4 + 1, LEN, dtype=jnp.int32)
    order = jnp.arange(LEN, dtype=jnp.int32)[None, :]
    return (order >= first_cut).astype(jnp.int32) + (order >= second_cut).astype(jnp.int32)


def levels(stream_key, dims, shards, least, largest):
    level, own = 1.0, jax.random.fold_in(stream_key, 6)
    for axis_at, blocks in shards:
        heights = jnp.exp(jax.random.uniform(jax.random.fold_in(own, axis_at), (blocks,), jnp.float32, least / len(shards), largest / len(shards)))
        level = level * jnp.repeat(heights, dims[axis_at] // blocks).reshape([-1 if axis == axis_at else 1 for axis in range(len(dims))])
    return level


def routed_block(key, own, number, rows, amount, top, bound, lean):
    ranking = jax.random.permutation(key, amount)
    heavy_load, common = shares(amount, rows * top, bound, lean, True), shares(amount, rows * top, bound, lean, False)
    places = jnp.arange(amount)

    def named(sizes, turn):
        used = int((sizes > 0).sum())
        fixed = max(1, used // 4)
        moved = fixed + (places - fixed + turn * (used - fixed)) % max(1, amount - fixed)
        return jnp.zeros((amount,), jnp.int32).at[ranking[jnp.where(places < fixed, places, moved)]].set(jnp.asarray(sizes, jnp.int32))

    sizes = jnp.where(number % 4 == 0, named(heavy_load, number // 4), named(common, number - number // 4 - 1))
    mixed = jax.random.permutation(jax.random.fold_in(own, 3), amount)
    giver, sink = mixed[0:amount // 2 * 2:2], mixed[1:amount // 2 * 2:2]
    margin = jnp.minimum(sizes[giver] - 1, bound - sizes[sink]) // 2
    margin = jnp.where((giver == ranking[0]) | (sink == ranking[0]) | (sizes[sink] == 0), 0, jnp.maximum(margin, 0))
    moved = jax.random.randint(jax.random.fold_in(own, 4), (amount // 2,), 0, 1 << 20) % (margin + 1)
    sizes = sizes.at[giver].add(-moved).at[sink].add(moved)
    items = jnp.searchsorted(jnp.cumsum(sizes), jnp.arange(rows * top), side="right").astype(jnp.int32)
    grid = items.reshape(top, rows).T
    grid = grid[jax.random.permutation(jax.random.fold_in(own, 1), rows)]
    turn = jax.random.randint(jax.random.fold_in(own, 2), (rows, 1), 0, top)
    return jnp.take_along_axis(grid, (jnp.arange(top)[None, :] + turn) % top, axis=1)


def shares(count, total, limit, slope, full):
    portions = [(1 << 20) // math.isqrt(grade ** slope) + 1 for grade in range(1, count + 1)]
    largest = limit if full else min(limit, max(-(-total // count), total * portions[0] // sum(portions)))
    least = 1 if total - largest >= count - 1 else 0
    holding, spare = [largest] + [least] * (count - 1), total - largest - least * (count - 1)
    while spare > 0:
        candidates = [i for i in range(1, count) if holding[i] < largest] or [i for i in range(1, count) if holding[i] < limit]
        mass, remaining = sum([portions[i] for i in candidates]), spare
        for i in candidates:
            more = min(limit - holding[i], max(1, remaining * portions[i] // mass), spare)
            holding[i] = holding[i] + more
            spare = spare - more
    return np.array(holding)


def scatter_about(stream_key, shape, spread, limit, pieces=(), held_as=jnp.bfloat16):
    level = levels(stream_key, shape, pieces, -0.22, 0.18) if pieces else 1.0
    values = jax.random.normal(stream_key, shape, jnp.float32) * spread * level
    return jnp.minimum(jnp.maximum(values, -limit), limit).astype(held_as)


def setup_inputs(seed: int = 0) -> dict:
    splits = jax.random.split(jax.random.key(seed), 17)
    block_input = scatter_about(splits[0], (SEQS, LEN, D), 1.0, 6.0, ((0, 32), (1, 4)))
    attn_norm_gain = jnp.clip(1.0 + 0.18 * jax.random.normal(splits[1], (D,), jnp.float32), 0.1, 1.9)
    query_proj = scatter_about(splits[2], (D, HEADS * HEAD), D ** -0.5, 0.1875)
    key_proj = scatter_about(splits[3], (D, KV_HEADS * HEAD), D ** -0.5, 0.1875)
    value_proj = scatter_about(splits[4], (D, KV_HEADS * HEAD), D ** -0.5, 0.1875)
    query_gain = jnp.clip(1.0 + 0.18 * jax.random.normal(splits[5], (HEAD,), jnp.float32), 0.1, 1.9)
    key_gain = jnp.clip(1.0 + 0.18 * jax.random.normal(splits[6], (HEAD,), jnp.float32), 0.1, 1.9)
    output_proj = scatter_about(splits[7], (HEADS * HEAD, D), (HEADS * HEAD // 32) ** -0.5, 1.0)
    ffn_norm_gain = jnp.clip(1.0 + 0.18 * jax.random.normal(splits[8], (D,), jnp.float32), 0.1, 1.9)
    router_proj = scatter_about(splits[9], (D, EXPERTS), (4 * D) ** -0.5, 0.09375)
    expert_routes_keys = jax.random.split(jax.random.fold_in(splits[10], 1), SEQS * LEN // TOK_DEV)
    expert_routes_turns = jax.random.permutation(jax.random.fold_in(splits[10], 3), SEQS * LEN // TOK_DEV)
    expert_routes = jax.vmap(lambda own, number: routed_block(jax.random.fold_in(splits[10], 2), own, number, TOK_DEV, EXPERTS, TOPK, CAP, 2))(expert_routes_keys, expert_routes_turns).reshape((SEQS, LEN, TOPK))
    document_ids = draw_document_ids(jax.random.fold_in(splits[16], 71), 0)
    expert_gate = scatter_about(splits[12], (EXPERTS, D, FF), D ** -0.5, 0.1875, ((0, 32),))
    expert_up = scatter_about(splits[13], (EXPERTS, D, FF), D ** -0.5, 0.1875, ((0, 32),))
    expert_down = scatter_about(splits[14], (EXPERTS, FF, D), (FF // 16) ** -0.5, 1.0, ((0, 32),))
    cotangent = scatter_about(splits[15], (SEQS, LEN, D), 1.0, 6.0, ((0, 32), (1, 4)))
    return dict(block_input=block_input, attn_norm_gain=attn_norm_gain, query_proj=query_proj, key_proj=key_proj, value_proj=value_proj, query_gain=query_gain, key_gain=key_gain, output_proj=output_proj, ffn_norm_gain=ffn_norm_gain, router_proj=router_proj, expert_routes=expert_routes, document_ids=document_ids, expert_gate=expert_gate, expert_up=expert_up, expert_down=expert_down, cotangent=cotangent)


@jax.custom_vjp
def low(v):
    return lax.optimization_barrier(v.astype(jnp.bfloat16)).astype(jnp.float32)

@jax.custom_vjp
def low_back(v):
    return v

def low_keep(v):
    return (low(v), None)

def low_pass(kept, grad):
    return (grad,)

def back_keep(v):
    return (v, None)

def back_low(kept, grad):
    return (low(grad),)
low.defvjp(low_keep, low_pass)
low_back.defvjp(back_keep, back_low)
epsilon = 1e-06
theta = 10000.0
masked = -1e+30
highest = lax.Precision.HIGHEST

def rms_scale(values, gain):
    return values * lax.rsqrt(lax.optimization_barrier(jnp.mean(values * values, axis=-1, keepdims=True)) + epsilon) * gain

def positions(doc_row):
    order = jnp.arange(doc_row.shape[0], dtype=jnp.int32)
    change = jnp.concatenate([jnp.ones((1,), jnp.bool_), doc_row[1:] != doc_row[:-1]])
    starts = lax.cummax(jnp.where(change, order, jnp.zeros_like(order)), axis=0)
    return order - starts

def rotate(values, position):
    half_width = values.shape[-1] // 2
    frequency = theta ** (-jnp.arange(half_width, dtype=jnp.float32) * 2.0 / values.shape[-1])
    angles = position.astype(jnp.float32)[:, None] * frequency[None, :]
    cosine = jnp.cos(angles)[:, None, :]
    sine_table = jnp.sin(angles)[:, None, :]
    first_half = values[..., :half_width]
    second = values[..., half_width:]
    return jnp.concatenate([first_half * cosine - second * sine_table, second * cosine + first_half * sine_table], axis=-1)

def softmax_rows(values):
    top_value = lax.optimization_barrier(jnp.max(values, axis=-1, keepdims=True))
    expo = jnp.exp(values - top_value)
    return expo / lax.optimization_barrier(jnp.sum(expo, axis=-1, keepdims=True))

def layer_seq(params, inputs, route_rows, doc_row):
    attn_gain, query_proj, key_proj, value_proj, query_gain, key_gain, output_proj, ffn_gain, router_proj, expert_gate, expert_up, expert_down = params
    length = inputs.shape[0]
    width = inputs.shape[1]
    normed = low(rms_scale(inputs, attn_gain))
    query_rows = low_back(jnp.dot(normed, query_proj, precision=highest)).reshape(length, HEADS, HEAD)
    key_rows = low_back(jnp.dot(normed, key_proj, precision=highest)).reshape(length, KV_HEADS, HEAD)
    value_rows = low(low_back(jnp.dot(normed, value_proj, precision=highest))).reshape(length, KV_HEADS, HEAD)
    position = positions(doc_row)
    query_rows = low(rotate(rms_scale(query_rows, query_gain), position))
    query_rows = query_rows.reshape(length, KV_HEADS, HEADS // KV_HEADS, HEAD)
    key_rows = low(rotate(rms_scale(key_rows, key_gain), position))
    scores = low_back(jnp.einsum('qkgd,skd->kgqs', query_rows, key_rows, precision=highest)) / math.sqrt(HEAD)
    order = jnp.arange(length, dtype=jnp.int32)
    allowed = (order[None, :] <= order[:, None]) & (doc_row[None, :] == doc_row[:, None])
    weights = low(softmax_rows(jnp.where(allowed, scores, masked)))
    attended = low(low_back(jnp.einsum('kgqs,skd->qkgd', weights, value_rows, precision=highest)))
    attended = attended.reshape(length, HEADS * HEAD)
    middle = inputs + low_back(jnp.dot(attended, output_proj, precision=highest))
    normed_two = low(rms_scale(middle, ffn_gain))
    logits = low_back(jnp.dot(normed_two, router_proj, precision=highest))
    gate_rows = softmax_rows(jnp.take_along_axis(logits, route_rows, axis=1))
    flat_routes = route_rows.reshape(-1)
    member = (flat_routes[:, None] == jnp.arange(EXPERTS, dtype=jnp.int32)[None, :]).astype(jnp.int32)
    rank = lax.optimization_barrier(jnp.sum((jnp.cumsum(member, axis=0, dtype=jnp.int32) - 1) * member, axis=1, dtype=jnp.int32))
    slots = N_DP * CAP
    slot_index = flat_routes * slots + rank
    slot_table = jnp.full((EXPERTS * slots,), length * TOPK, jnp.int32)
    slot_table = slot_table.at[slot_index].set(jnp.arange(length * TOPK, dtype=jnp.int32))
    padded = jnp.concatenate([normed_two, jnp.zeros((1, width), normed_two.dtype)], axis=0)
    received = low_back(padded[slot_table // TOPK].reshape(EXPERTS, slots, width))
    gate_act = low_back(jnp.einsum('esd,edf->esf', received, expert_gate, precision=highest))
    up_act = low_back(jnp.einsum('esd,edf->esf', received, expert_up, precision=highest))
    hidden = low(gate_act / (1.0 + jnp.exp(-gate_act)) * up_act)
    result = low(low_back(jnp.einsum('esf,efd->esd', hidden, expert_down, precision=highest)))
    picked = result.reshape(EXPERTS * slots, width)[slot_index].reshape(length, TOPK, width)
    return middle + jnp.einsum('nk,nkd->nd', gate_rows, picked, precision=highest)

def forward(params, inputs, routes, documents):

    def one_sequence(item):
        return jax.checkpoint(layer_seq)(params, item[0], item[1], item[2])
    return lax.map(one_sequence, (inputs, routes, documents))

def reference(block_input, attn_norm_gain, query_proj, key_proj, value_proj, query_gain, key_gain, output_proj, ffn_norm_gain, router_proj, expert_routes, document_ids, expert_gate, expert_up, expert_down, cotangent):
    params = (attn_norm_gain.astype(jnp.float32), query_proj.astype(jnp.float32), key_proj.astype(jnp.float32), value_proj.astype(jnp.float32), query_gain.astype(jnp.float32), key_gain.astype(jnp.float32), output_proj.astype(jnp.float32), ffn_norm_gain.astype(jnp.float32), router_proj.astype(jnp.float32), expert_gate.astype(jnp.float32), expert_up.astype(jnp.float32), expert_down.astype(jnp.float32))
    inputs = block_input.astype(jnp.float32)

    def whole(weights, values):
        return forward(weights, values, expert_routes, document_ids)
    output, pullback = jax.vjp(whole, params, inputs)
    gradient, input_grad = pullback(cotangent.astype(jnp.float32))
    return (output.astype(jnp.bfloat16), input_grad, gradient[0], gradient[1], gradient[2], gradient[3], gradient[4], gradient[5], gradient[6], gradient[7], gradient[8], gradient[9], gradient[10], gradient[11])
```

```python
import jax
import jax.numpy as jnp
from jax import lax
from jax.experimental import pallas as pl
from jax.experimental.pallas import tpu as pltpu
from jax.sharding import PartitionSpec as P

CAP = 80
SIDE = 4
TOP = 8
BF = jnp.bfloat16
F32 = jnp.float32
MIB = 1024 * 1024

epsilon = 1e-06
theta = 10000.0
masked = -1e30


def place(x, y, core):
    return (x * SIDE + y) * 2 + core


def step_pairs(dx, dy, flip=0):
    pairs = []
    for x in range(SIDE):
        for y in range(SIDE):
            for core in range(2):
                there = place((x + dx) % SIDE, (y + dy) % SIDE, core ^ flip)
                pairs.append((place(x, y, core), there))
    return pairs


def along_x(value, step):
    return lax.ppermute(value, "expert", step_pairs(step, 0))


def along_y(value, step):
    return lax.ppermute(value, "expert", step_pairs(0, step))


def along_z(value, step):
    return lax.ppermute(value, "dp", [(i, (i + step) % SIDE) for i in range(SIDE)])


def swap_core(value):
    return lax.ppermute(value, "expert", step_pairs(0, 0, 1))


def plane_groups():
    return [[2 * chip + core for chip in range(SIDE * SIDE)] for core in range(2)]


def tied(*values):
    return lax.optimization_barrier(values)


def ring_start(parts, move):
    half = parts.shape[1] // 2
    return move(parts[2, :half], 1), move(parts[2, half:], -1)


def ring_middle(parts, first, move):
    half = parts.shape[1] // 2
    ahead, behind = first
    up = jnp.concatenate([parts[1, :half] + ahead, parts[1, half:]], axis=0)
    down = jnp.concatenate([parts[3, :half], parts[3, half:] + behind], axis=0)
    return move(up, 1), move(down, -1)


def ring_end(parts, second):
    return parts[0].astype(F32) + second[0].astype(F32) + second[1].astype(F32)


def plane_sum(part_a, part_b):
    for move_a, move_b in ((along_x, along_y), (along_y, along_x)):
        first_a, first_b = ring_start(part_a, move_a), ring_start(part_b, move_b)
        second_a = ring_middle(part_a, first_a, move_a)
        second_b = ring_middle(part_b, first_b, move_b)
        part_a, part_b = ring_end(part_a, second_a), ring_end(part_b, second_b)
        if part_a.ndim == 3:
            part_a, part_b = part_a.astype(BF), part_b.astype(BF)
    return part_a, part_b


def block_at(whole, index, rows):
    return lax.dynamic_slice_in_dim(whole, (index % SIDE) * rows, rows, axis=0)


def scatter_sum(whole, tail, here, move):
    rows = whole.shape[0] // SIDE
    total = jnp.concatenate([block_at(whole, here, rows), tail], axis=0).astype(F32)
    for r, step in ((1, 1), (2, 2), (3, -1)):
        send = jnp.concatenate([block_at(whole, here + r, rows), tail], axis=0)
        total = total + move(send, step).astype(F32)
    total = total.astype(BF)
    return total[:rows], total[rows:]


def gather_rows(part, here, move):
    rows = part.shape[0]
    whole = jnp.zeros((SIDE * rows,) + part.shape[1:], part.dtype)
    pieces = [part, move(part, -1), move(part, 2), move(part, 1)]
    for r, piece in enumerate(pieces):
        whole = lax.dynamic_update_slice_in_dim(whole, piece, ((here + r) % SIDE) * rows, 0)
    return whole


def nt(a, b):
    return lax.dot_general(a, b, (((1,), (1,)), ((), ())), preferred_element_type=F32)


def tn(a, b):
    return lax.dot_general(a, b, (((0,), (0,)), ((), ())), preferred_element_type=F32)


def nn(a, b):
    return jnp.dot(a, b, preferred_element_type=F32)


def head_mean(values, head):
    n = values.shape[1]
    same = lax.broadcasted_iota(jnp.int32, (n, n), 0) // head == (
        lax.broadcasted_iota(jnp.int32, (n, n), 1) // head
    )
    ones = jnp.where(same, 1.0, 0.0).astype(BF)
    high = values.astype(BF)
    rest = values - high.astype(F32)
    middle = rest.astype(BF)
    low = (rest - middle.astype(F32)).astype(BF)
    return (nn(high, ones) + nn(middle, ones) + nn(low, ones)) * (1.0 / head)


def turn(values, cosine, sine, head):
    half = head // 2
    pieces = []
    lane = lax.broadcasted_iota(jnp.int32, (values.shape[0], 128), 1) % head
    for at in range(0, values.shape[1], 128):
        piece = values[:, at : at + 128]
        other = jnp.where(
            lane < half, pltpu.roll(piece, 128 - half, 1), pltpu.roll(piece, half, 1)
        )
        pieces.append(piece * cosine + other * sine)
    return pieces[0] if len(pieces) == 1 else jnp.concatenate(pieces, axis=1)


def allowed_keys(start, block, rows):
    length = (block + 1) * rows
    key = lax.broadcasted_iota(jnp.int32, (rows, length), 1)
    query = lax.broadcasted_iota(jnp.int32, (rows, length), 0) + block * rows
    return (key <= query) & (key >= start)


def attend_kernel(
    at_ref,
    x0_ref,
    x1_ref,
    x2_ref,
    x3_ref,
    gain_ref,
    wq_ref,
    wk_ref,
    wv_ref,
    qgain_ref,
    kgain_ref,
    cos_ref,
    sin_ref,
    start_ref,
    normed_ref,
    q_ref,
    k_ref,
    v_ref,
    qraw_ref,
    kraw_ref,
    out_ref,
    head,
):
    z = at_ref[0]
    rows = x0_ref.shape[0]
    for r, x_ref in enumerate((x0_ref, x1_ref, x2_ref, x3_ref)):
        here = pl.ds(pl.multiple_of(lax.rem(z - r + SIDE, SIDE) * rows, rows), rows)
        x = x_ref[...].astype(F32)
        scale = lax.rsqrt(jnp.mean(x * x, axis=-1, keepdims=True) + epsilon)
        normed = (x * scale * gain_ref[...]).astype(BF)
        normed_ref[here] = normed
        cosine, sine = cos_ref[here], sin_ref[here]
        q_raw = nn(normed, wq_ref[...])
        k_raw = nn(normed, wk_ref[...])
        v_ref[here] = nn(normed, wv_ref[...]).astype(BF)
        qraw_ref[here] = q_raw
        kraw_ref[here] = k_raw
        q = q_raw * lax.rsqrt(head_mean(q_raw * q_raw, head) + epsilon) * qgain_ref[...]
        k = k_raw * lax.rsqrt(head_mean(k_raw * k_raw, head) + epsilon) * kgain_ref[...]
        q_ref[here] = turn(q, cosine, sine, head).astype(BF) * (head**-0.5)
        k_ref[here] = turn(k, cosine, sine, head).astype(BF)
    for i in range(SIDE):
        length = (i + 1) * rows
        keep = allowed_keys(start_ref[i * rows : (i + 1) * rows], i, rows)
        outs = []
        for h in range(q_ref.shape[1] // head):
            j = h // 2
            q = q_ref[i * rows : (i + 1) * rows, h * head : (h + 1) * head]
            k = k_ref[:length, j * head : (j + 1) * head]
            v = v_ref[:length, j * head : (j + 1) * head]
            expo = jnp.where(keep, jnp.exp(nt(q, k)), 0.0)
            total = jnp.sum(expo, axis=1, keepdims=True)
            outs.append(nn(expo.astype(BF), v) / total)
        out_ref[lax.rem(i - z + SIDE, SIDE)] = jnp.concatenate(outs, axis=1).astype(BF)


def attend(at, x_rel, gain, query_proj, key_proj, value_proj, qgain, kgain, cosine, sine, start):
    rows, width = x_rel[0].shape
    length = SIDE * rows
    head = qgain.shape[0]
    q_cols, k_cols = query_proj.shape[1] // SIDE, key_proj.shape[1] // SIDE

    def whole(shape):
        return pl.BlockSpec(shape, lambda g, at: (0,) * len(shape))

    def columns(cols):
        return pl.BlockSpec((width, cols), lambda g, at: (0, at[0]))

    shapes = [
        ((length, width), BF),
        ((length, q_cols), BF),
        ((length, k_cols), BF),
        ((length, k_cols), BF),
        ((length, q_cols), F32),
        ((length, k_cols), F32),
        ((SIDE, rows, q_cols), BF),
    ]

    def kernel(*refs):
        attend_kernel(*refs, head=head)

    return pl.pallas_call(
        kernel,
        grid_spec=pltpu.PrefetchScalarGridSpec(
            num_scalar_prefetch=1,
            grid=(1,),
            in_specs=[whole((rows, width))] * SIDE
            + [whole((1, width)), columns(q_cols), columns(k_cols), columns(k_cols)]
            + [whole((1, q_cols)), whole((1, k_cols))]
            + [whole((length, 128)), whole((length, 128)), whole((length, 1))],
            out_specs=[whole(shape) for shape, _ in shapes],
        ),
        out_shape=[jax.ShapeDtypeStruct(shape, dtype) for shape, dtype in shapes],
        compiler_params=pltpu.CompilerParams(vmem_limit_bytes=48 * MIB),
        cost_estimate=pl.CostEstimate(
            flops=6_000_000_000, bytes_accessed=12_000_000, transcendentals=4_000_000
        ),
        name="attend",
    )(
        at,
        *x_rel,
        gain[None],
        query_proj,
        key_proj,
        value_proj,
        jnp.tile(qgain, q_cols // head)[None],
        jnp.tile(kgain, k_cols // head)[None],
        cosine,
        sine,
        start,
    )


def norm_back(raw, upstream, gain, head):
    scale = lax.rsqrt(head_mean(raw * raw, head) + epsilon)
    gain_grad = jnp.sum(upstream * raw * scale, axis=0, keepdims=True)
    weighted = upstream * gain
    inner = head_mean(weighted * raw, head)
    return scale * weighted - raw * (scale * scale * scale) * inner, gain_grad


def attend_back_kernel(
    at_ref,
    d0_ref,
    d1_ref,
    d2_ref,
    d3_ref,
    q_ref,
    k_ref,
    v_ref,
    qraw_ref,
    kraw_ref,
    qgain_ref,
    kgain_ref,
    cos_ref,
    sin_ref,
    start_ref,
    dqkv_ref,
    gains_ref,
    do_scr,
    dk_scr,
    dv_scr,
    head,
):
    z = at_ref[0]
    rows = d0_ref.shape[0]
    q_cols, k_cols = q_ref.shape[1], k_ref.shape[1]
    for r, d_ref in enumerate((d0_ref, d1_ref, d2_ref, d3_ref)):
        here = pl.ds(pl.multiple_of(lax.rem(z - r + SIDE, SIDE) * rows, rows), rows)
        do_scr[here] = d_ref[...]
    gains_ref[...] = jnp.zeros_like(gains_ref)
    for i in reversed(range(SIDE)):
        length = (i + 1) * rows
        here = slice(i * rows, (i + 1) * rows)
        keep = allowed_keys(start_ref[here], i, rows)
        d_queries = []
        for j in range(k_cols // head):
            k = k_ref[:length, j * head : (j + 1) * head]
            v = v_ref[:length, j * head : (j + 1) * head]
            d_key, d_value = 0.0, 0.0
            for h in (2 * j, 2 * j + 1):
                q = q_ref[here, h * head : (h + 1) * head]
                grad = do_scr[here, h * head : (h + 1) * head]
                expo = jnp.where(keep, jnp.exp(nt(q, k)), 0.0)
                probs = expo * (1.0 / jnp.sum(expo, axis=1, keepdims=True))
                d_probs = nt(grad, v)
                inner = jnp.sum(probs * d_probs, axis=1, keepdims=True)
                d_scores = (probs * (d_probs - inner)).astype(BF)
                d_queries.append(nn(d_scores, k) * (head**-0.5))
                d_key = d_key + tn(d_scores, q)
                d_value = d_value + tn(probs.astype(BF), grad)
            if i == SIDE - 1:
                dk_scr[j] = d_key
                dv_scr[j] = d_value
            else:
                dk_scr[j, :length] += d_key
                dv_scr[j, :length] += d_value
        d_query = jnp.concatenate(d_queries, axis=1)
        d_query = turn(d_query, cos_ref[here], -sin_ref[here], head)
        d_raw, d_gain = norm_back(qraw_ref[here], d_query, qgain_ref[...], head)
        dqkv_ref[here, :q_cols] = d_raw.astype(BF)
        gains_ref[0:1] += d_gain
        d_key = jnp.concatenate([dk_scr[0, here], dk_scr[1, here]], axis=1)
        d_key = turn(d_key, cos_ref[here], -sin_ref[here], head)
        d_raw, d_gain = norm_back(kraw_ref[here], d_key, kgain_ref[...], head)
        dqkv_ref[here, q_cols : q_cols + k_cols] = d_raw.astype(BF)
        gains_ref[1:2, :k_cols] += d_gain
        d_value = jnp.concatenate([dv_scr[0, here], dv_scr[1, here]], axis=1)
        dqkv_ref[here, q_cols + k_cols :] = d_value.astype(BF)


def attend_back(at, d_rel, q, k, v, q_raw, k_raw, qgain, kgain, cosine, sine, start):
    rows = d_rel[0].shape[0]
    length, q_cols = q.shape
    k_cols = k.shape[1]
    head = qgain.shape[0]

    def whole(shape):
        return pl.BlockSpec(shape, lambda g, at: (0,) * len(shape))

    def kernel(*refs):
        attend_back_kernel(*refs, head=head)

    operands = [
        *d_rel,
        q,
        k,
        v,
        q_raw,
        k_raw,
        jnp.tile(qgain, q_cols // head)[None],
        jnp.tile(kgain, k_cols // head)[None],
        cosine,
        sine,
        start,
    ]
    shapes = [((length, q_cols + 2 * k_cols), BF), ((8, q_cols), F32)]
    return pl.pallas_call(
        kernel,
        grid_spec=pltpu.PrefetchScalarGridSpec(
            num_scalar_prefetch=1,
            grid=(1,),
            in_specs=[whole(a.shape) for a in operands],
            out_specs=[whole(shape) for shape, _ in shapes],
            scratch_shapes=[
                pltpu.VMEM((length, q_cols), BF),
                pltpu.VMEM((k_cols // head, length, head), F32),
                pltpu.VMEM((k_cols // head, length, head), F32),
            ],
        ),
        out_shape=[jax.ShapeDtypeStruct(shape, dtype) for shape, dtype in shapes],
        compiler_params=pltpu.CompilerParams(vmem_limit_bytes=48 * MIB),
        cost_estimate=pl.CostEstimate(
            flops=8_000_000_000, bytes_accessed=8_000_000, transcendentals=4_000_000
        ),
        name="attend_back",
    )(at, *operands)


def moe_kernel(
    at_ref,
    rows_ref,
    cot_ref,
    router_ref,
    gate_ref,
    up_ref,
    down_ref,
    out_a_ref,
    out_b_ref,
    back_a_ref,
    back_b_ref,
    x_ref,
    dgate_ref,
    dup_ref,
    hidden_ref,
    slot_ref,
    pick_scr,
    up_scr,
    gate_scr,
    dgs_scr,
    o_scr,
    b_scr,
):
    tokens = rows_ref.shape[2]
    width = rows_ref.shape[3]
    half = width // 2
    experts = router_ref.shape[0]
    y_here, chip = at_ref[2], at_ref[3]
    pick_iota = lax.broadcasted_iota(jnp.int32, (CAP, tokens), 0).astype(F32)
    expert_iota = lax.broadcasted_iota(jnp.int32, (experts, tokens), 0).astype(F32)
    chip_row = lax.broadcasted_iota(jnp.int32, (SIDE * SIDE, half), 0) == chip
    tri = (
        lax.broadcasted_iota(jnp.int32, (tokens, tokens), 0)
        <= lax.broadcasted_iota(jnp.int32, (tokens, tokens), 1)
    ).astype(BF)
    mine = [at_ref[4 + j].astype(F32) for j in range(2)]
    members, gates = [], []
    for s in range(SIDE):
        rows = rows_ref[0, s]
        routes = cot_ref[0, s, tokens : tokens + 16, :tokens].astype(F32)
        logits = nt(router_ref[...], rows)
        chosen = expert_iota == routes[0:1]
        for k in range(1, TOP):
            chosen = chosen | (expert_iota == routes[k : k + 1])
        top = jnp.max(jnp.where(chosen, logits, masked), axis=0, keepdims=True)
        expo = jnp.where(chosen, jnp.exp(jnp.minimum(logits - top, 0.0)), 0.0)
        share = expo / jnp.sum(expo, axis=0, keepdims=True)
        for j in range(2):
            picked = expert_iota == mine[j]
            gates.append(jnp.sum(jnp.where(picked, share, 0.0), axis=0, keepdims=True))
            members.append(jnp.sum(jnp.where(picked & chosen, 1.0, 0.0), axis=0, keepdims=True))
    member_all = jnp.concatenate(members, axis=0)
    rank_all = nn(member_all.astype(BF), tri)
    rank_all = jnp.where(member_all > 0.5, rank_all - 1.0, -1.0)
    for s in range(SIDE):
        for j in range(2):
            n = s * 2 + j
            hit = pick_iota == rank_all[n : n + 1]
            pick_scr[s, j * CAP : (j + 1) * CAP] = jnp.where(hit, 1.0, 0.0).astype(BF)
            gate_scr[j, s * CAP : (s + 1) * CAP] = jnp.sum(
                jnp.where(hit, gates[n], 0.0), axis=1, keepdims=True
            )
        pick = pick_scr[s]
        took = nn(pick, rows_ref[0, s]).astype(BF)
        took_up = nn(pick, cot_ref[0, s, :tokens]).astype(BF)
        for j in range(2):
            x_ref[j, s * CAP : (s + 1) * CAP] = took[j * CAP : (j + 1) * CAP]
            up_scr[j, s * CAP : (s + 1) * CAP] = took_up[j * CAP : (j + 1) * CAP]
    for j in range(2):
        x = x_ref[j]
        gate_act = nn(x, gate_ref[j])
        up_act = nn(x, up_ref[j])
        sig = 1.0 / (1.0 + jnp.exp(-gate_act))
        silu = gate_act * sig
        hidden = (silu * up_act).astype(BF)
        hidden_ref[j] = hidden
        upstream = up_scr[j].astype(F32)
        gate_col = gate_scr[j]
        slot = (gate_col * upstream).astype(BF)
        slot_ref[j] = slot
        result = nn(hidden, down_ref[j]).astype(BF).astype(F32)
        dgs_scr[j] = jnp.sum(upstream * result, axis=1, keepdims=True)
        gated = (gate_col * result).astype(BF)
        d_hidden = nt(slot, down_ref[j])
        d_gate = (d_hidden * up_act * (sig + silu * (1.0 - sig))).astype(BF)
        d_up = (d_hidden * silu).astype(BF)
        dgate_ref[j] = d_gate
        dup_ref[j] = d_up
        d_rows = (nt(d_gate, gate_ref[j]) + nt(d_up, up_ref[j])).astype(BF)
        for s in range(SIDE):
            o_scr[s, j * CAP : (j + 1) * CAP] = gated[s * CAP : (s + 1) * CAP]
            b_scr[s, j * CAP : (j + 1) * CAP] = d_rows[s * CAP : (s + 1) * CAP]
    for s in range(SIDE):
        dy = lax.rem(s - y_here + SIDE, SIDE)
        pick = pick_scr[s]
        back = tn(pick, b_scr[s]).astype(BF)
        back_a_ref[0, dy, :tokens] = back[:, :half]
        back_b_ref[dy, 0, :tokens] = back[:, half:]
        out = tn(pick, o_scr[s]).astype(BF)
        out_a_ref[0, dy] = out[:, :half]
        out_b_ref[dy, 0] = out[:, half:]
        found = []
        for j in range(2):
            hit = pick_iota == rank_all[s * 2 + j : s * 2 + j + 1]
            col = dgs_scr[j, s * CAP : (s + 1) * CAP]
            found.append(jnp.sum(jnp.where(hit, col, 0.0), axis=0, keepdims=True))
        found = jnp.where(chip_row, jnp.concatenate(found, axis=1), 0.0)
        high = found.astype(BF)
        back_a_ref[0, dy, tokens:] = high
        back_b_ref[dy, 0, tokens:] = (found - high.astype(F32)).astype(BF)


def moe(at, rows, cot, router_t, gate, up, down):
    _, _, tokens, width = rows.shape
    padded = cot.shape[2]
    ff = gate.shape[2]
    slots = SIDE * CAP
    half = width // 2

    def whole(shape):
        return pl.BlockSpec(shape, lambda g, at: (0,) * len(shape))

    def source(g, at):
        return (at[1] + 2 + g) % SIDE

    def first(g, at):
        return ((2 + g) % SIDE, 0, 0, 0)

    def second(g, at):
        return (0, (2 + g) % SIDE, 0, 0)

    kept = [width, ff, ff, ff, width]
    return pl.pallas_call(
        moe_kernel,
        grid_spec=pltpu.PrefetchScalarGridSpec(
            num_scalar_prefetch=1,
            grid=(SIDE,),
            in_specs=[
                pl.BlockSpec((1, SIDE, tokens, width), lambda g, at: (source(g, at), 0, 0, 0)),
                pl.BlockSpec((1, SIDE, padded, width), lambda g, at: (source(g, at), 0, 0, 0)),
                whole(router_t.shape),
                whole(gate.shape),
                whole(up.shape),
                whole(down.shape),
            ],
            out_specs=[
                pl.BlockSpec((1, SIDE, tokens, half), first),
                pl.BlockSpec((SIDE, 1, tokens, half), second),
                pl.BlockSpec((1, SIDE, padded, half), first),
                pl.BlockSpec((SIDE, 1, padded, half), second),
            ]
            + [pl.BlockSpec((2, slots, n), lambda g, at: (0, g, 0)) for n in kept],
            scratch_shapes=[
                pltpu.VMEM((SIDE, 2 * CAP, tokens), BF),
                pltpu.VMEM((2, slots, width), BF),
                pltpu.VMEM((2, slots, 1), F32),
                pltpu.VMEM((2, slots, 1), F32),
                pltpu.VMEM((SIDE, 2 * CAP, width), BF),
                pltpu.VMEM((SIDE, 2 * CAP, width), BF),
            ],
        ),
        out_shape=[jax.ShapeDtypeStruct((SIDE, SIDE, tokens, half), BF)] * 2
        + [jax.ShapeDtypeStruct((SIDE, SIDE, padded, half), BF)] * 2
        + [jax.ShapeDtypeStruct((2, SIDE * slots, n), BF) for n in kept],
        compiler_params=pltpu.CompilerParams(vmem_limit_bytes=60 * MIB),
        cost_estimate=pl.CostEstimate(
            flops=22_000_000_000, bytes_accessed=60_000_000, transcendentals=0
        ),
        name="moe",
    )(at, rows, cot, router_t, gate, up, down)


def rms_apply(values, gain):
    scale = lax.rsqrt(jnp.mean(values * values, axis=-1, keepdims=True) + epsilon)
    return (values * scale * gain, scale)


def rms_back(values, scale, gain, upstream):
    weighted = upstream * gain
    inner = jnp.mean(weighted * values, axis=-1, keepdims=True)
    return scale * weighted - values * (scale * scale * scale) * inner


def body(
    block_input,
    attn_norm_gain,
    query_proj,
    key_proj,
    value_proj,
    query_gain,
    key_gain,
    output_proj,
    ffn_norm_gain,
    router_proj,
    expert_routes,
    document_ids,
    expert_gate,
    expert_up,
    expert_down,
    cotangent,
):
    tokens, width = block_input.shape[1:]
    head = query_gain.shape[0]
    experts_all = router_proj.shape[1]
    z = lax.axis_index("dp")
    expert_at = lax.axis_index("expert")
    chip, core = expert_at // 2, expert_at % 2
    x_at, y_at = chip // SIDE, chip % SIDE
    at = jnp.stack([z, x_at, y_at, chip, expert_at, expert_at + 1 - 2 * core]).astype(jnp.int32)

    own = block_input[0]
    x_rel = [own, along_z(own, 1), along_z(own, 2), along_z(own, -1)]
    routes = expert_routes[0]
    route_rows = jnp.full((16, width), -1.0, BF)
    route_rows = lax.dynamic_update_slice(route_rows, routes.T.astype(BF), (0, 0))
    cot_all = lax.all_gather(
        jnp.concatenate([cotangent[0], route_rows], axis=0),
        "expert",
        axis_index_groups=plane_groups(),
    ).reshape(SIDE, SIDE, tokens + 16, width)

    doc = document_ids[0]
    below_one = jnp.sum((doc < 1).astype(jnp.int32))
    below_two = jnp.sum((doc < 2).astype(jnp.int32))
    start = jnp.where(doc < 1, 0, jnp.where(doc < 2, below_one, below_two)).astype(jnp.int32)
    position = (jnp.arange(doc.shape[0], dtype=jnp.int32) - start).astype(F32)
    frequency = theta ** (-jnp.arange(head // 2, dtype=F32) * 2.0 / head)
    angles = position[:, None] * frequency[None, :]
    cosine, sine = jnp.cos(angles), jnp.sin(angles)
    cosine = jnp.tile(cosine, (1, 4))
    sine = jnp.tile(jnp.concatenate([-sine, sine], axis=1), (1, 2))
    start = start[:, None]

    normed_all, q, k, v, q_raw, k_raw, out_rel = attend(
        at,
        x_rel,
        attn_norm_gain,
        query_proj,
        key_proj,
        value_proj,
        query_gain,
        key_gain,
        cosine,
        sine,
        start,
    )
    q_cols, k_cols = q.shape[1], k.shape[1]

    def from_heads(pieces):
        whole = jnp.zeros((tokens, SIDE, pieces[0].shape[1]), pieces[0].dtype)
        for r, piece in enumerate(pieces):
            whole = lax.dynamic_update_slice(whole, piece[:, None], (0, (z - r) % SIDE, 0))
        return whole

    attended = from_heads(
        [out_rel[0], along_z(out_rel[1], 1), along_z(out_rel[2], 2), along_z(out_rel[3], -1)]
    ).reshape(tokens, SIDE * q_cols)
    inputs = own.astype(F32)
    middle = inputs + nn(attended, output_proj)
    normed_two, scale_two = rms_apply(middle, ffn_norm_gain)
    normed_two = normed_two.astype(BF)
    rows_all = lax.all_gather(
        normed_two, "expert", axis_index_groups=plane_groups()
    ).reshape(SIDE, SIDE, tokens, width)
    gate_two = jnp.concatenate([expert_gate, swap_core(expert_gate)], axis=0)
    up_two = jnp.concatenate([expert_up, swap_core(expert_up)], axis=0)
    down_two = jnp.concatenate([expert_down, swap_core(expert_down)], axis=0)
    out_a, out_b, back_a, back_b, kept_x, kept_dg, kept_du, kept_h, kept_s = moe(
        at, rows_all, cot_all, router_proj.T, gate_two, up_two, down_two
    )

    logits = nn(normed_two, router_proj)
    experts = jnp.arange(experts_all, dtype=jnp.int32)
    chosen = jnp.any(routes[:, :, None] == experts[None, None, :], axis=1)
    logits = jnp.where(chosen, logits, masked)
    expo = jnp.where(chosen, jnp.exp(logits - jnp.max(logits, axis=-1, keepdims=True)), 0.0)
    gate_rows = expo / jnp.sum(expo, axis=-1, keepdims=True)

    sum_a, sum_b = plane_sum(back_a, back_b)
    back_sum = jnp.concatenate([sum_a[:tokens], sum_b[:tokens]], axis=1)
    d_gates = (sum_a[tokens:] + sum_b[tokens:]).reshape(SIDE * SIDE, 2, tokens)
    d_gates = jnp.where(core == 0, d_gates, d_gates[:, ::-1]).reshape(experts_all, tokens).T
    d_gates = jnp.where(chosen, d_gates, 0.0)

    def slots_grad(a, b):
        return jnp.einsum("jrd,jrf->jdf", a, b, preferred_element_type=F32).astype(BF)

    whole_w = jnp.stack(
        [slots_grad(kept_x, kept_dg), slots_grad(kept_x, kept_du), slots_grad(kept_s, kept_h)],
        axis=1,
    )
    whole_w = (whole_w[0].astype(F32) + swap_core(whole_w[1]).astype(F32)).astype(BF)
    expert_sum = lax.psum_scatter(whole_w, "dp", scatter_dimension=1, tiled=True).astype(F32)
    gate_grad, up_grad = expert_sum[0:1], expert_sum[1:2]
    down_grad = jnp.transpose(expert_sum[2:3], (0, 2, 1))

    upstream = cotangent[0].astype(F32)
    d_chosen = gate_rows * (d_gates - jnp.sum(gate_rows * d_gates, axis=-1, keepdims=True))
    d_logits = d_chosen.astype(BF)
    router_local = tn(d_logits, normed_two)
    d_normed_two = back_sum + nt(d_logits, router_proj)
    ffn_gain_local = jnp.sum(d_normed_two * middle * scale_two, axis=0)
    d_middle = upstream + rms_back(middle, scale_two, ffn_norm_gain, d_normed_two)
    d_branch = d_middle.astype(BF)
    d_attended = nt(d_branch, output_proj).astype(BF).reshape(tokens, SIDE, q_cols)

    def heads_of(r):
        return lax.dynamic_index_in_dim(d_attended, (z + r) % SIDE, axis=1, keepdims=False)

    d_rel = [heads_of(0)] + [along_z(heads_of(r), s) for r, s in ((1, 1), (2, 2), (3, -1))]
    dqkv, gains = attend_back(
        at, d_rel, q, k, v, q_raw, k_raw, query_gain, key_gain, cosine, sine, start
    )
    output_local = tn(attended, d_branch)
    early = jnp.concatenate(
        [output_local, router_local, jnp.pad(ffn_gain_local[None], ((0, 15), (0, 0)))], axis=0
    )
    early = lax.psum(early.astype(BF), ("dp", "expert"))

    local = tn(normed_all, dqkv).astype(BF)
    tail = jnp.concatenate([gains[0], gains[1]])
    tail = jnp.pad(tail[None], ((0, 15), (0, 0))).astype(BF)
    half = width // 2
    mine = lax.dynamic_slice_in_dim(local, core * half, half, axis=0)
    other = lax.dynamic_slice_in_dim(local, (1 - core) * half, half, axis=0)
    got = swap_core(jnp.concatenate([other, tail], axis=0)).astype(F32)
    part = (mine.astype(F32) + got[:half]).astype(BF)
    tail = (tail.astype(F32) + got[half:]).astype(BF)
    part, tail = scatter_sum(part, tail, x_at, along_x)
    part, tail = scatter_sum(part, tail, y_at, along_y)
    part = gather_rows(part, y_at, along_y)
    part = gather_rows(part, x_at, along_x)
    part = jnp.concatenate([part, tail], axis=0)
    blocks = gather_heads(part, z)
    tails = jnp.sum(blocks[:, half].astype(F32), axis=0)
    query_gain_sum = jnp.sum(tails[:q_cols].reshape(-1, head), axis=0)
    key_gain_sum = jnp.sum(tails[q_cols : q_cols + k_cols].reshape(-1, head), axis=0)
    blocks = blocks[:, :half]
    blocks_other = swap_core(blocks)
    both = jnp.where(
        core == 0, jnp.stack([blocks, blocks_other]), jnp.stack([blocks_other, blocks])
    )
    both = both.transpose(0, 2, 1, 3).reshape(width, SIDE, q_cols + 2 * k_cols).astype(F32)
    query_sum = both[:, :, :q_cols].reshape(width, -1)
    key_sum = both[:, :, q_cols : q_cols + k_cols].reshape(width, -1)
    value_sum = both[:, :, q_cols + k_cols :].reshape(width, -1)
    attn_gain_sum = (
        jnp.sum(query_sum * query_proj.astype(F32), axis=1)
        + jnp.sum(key_sum * key_proj.astype(F32), axis=1)
        + jnp.sum(value_sum * value_proj.astype(F32), axis=1)
    ) / attn_norm_gain

    def block_of(r):
        return block_at(dqkv, z + r, tokens)

    back = from_heads(
        [block_of(0)] + [along_z(block_of(r), s) for r, s in ((1, 1), (2, 2), (3, -1))]
    )
    d_query = back[:, :, :q_cols].reshape(tokens, -1)
    d_key = back[:, :, q_cols : q_cols + k_cols].reshape(tokens, -1)
    d_value = back[:, :, q_cols + k_cols :].reshape(tokens, -1)
    d_normed = nt(d_query, query_proj) + nt(d_key, key_proj) + nt(d_value, value_proj)
    scale_one = lax.rsqrt(jnp.mean(inputs * inputs, axis=-1, keepdims=True) + epsilon)
    input_grad = d_middle + rms_back(inputs, scale_one, attn_norm_gain, d_normed)

    out_a, out_b, _ = tied(out_a, out_b, d_branch)
    out_a, out_b = plane_sum(out_a, out_b)
    block_output = (middle + jnp.concatenate([out_a, out_b], axis=1)).astype(BF)

    early = early.astype(F32)
    return (
        block_output[None],
        input_grad[None],
        attn_gain_sum,
        query_sum,
        key_sum,
        value_sum,
        query_gain_sum,
        key_gain_sum,
        early[:width],
        early[width + experts_all],
        early[width : width + experts_all].T,
        gate_grad,
        up_grad,
        down_grad,
    )


def gather_heads(part, z):
    pieces = [part, along_z(part, 1), along_z(part, 2), along_z(part, -1)]
    whole = jnp.zeros((SIDE,) + part.shape, part.dtype)
    for r, piece in enumerate(pieces):
        whole = lax.dynamic_update_index_in_dim(whole, piece, (z - r) % SIDE, 0)
    return whole


def solution(mesh):
    tokens = P("expert", "dp", None)
    experts = P("expert", None, None)
    return jax.shard_map(
        body,
        mesh=mesh,
        in_specs=(tokens,)
        + (P(),) * 9
        + (tokens, P("expert", None), experts, experts, experts, tokens),
        out_specs=(tokens, tokens)
        + (P(),) * 9
        + (tokens, tokens, P("expert", None, "dp")),
        check_vma=False,
    )
```

```python
import jax
import jax.numpy as jnp
from jax import lax
from jax.experimental import pallas as pl
from jax.experimental.pallas import tpu as pltpu
from jax.sharding import PartitionSpec as P

CAP = 80
SIDE = 4
TOP = 8
BF = jnp.bfloat16
F32 = jnp.float32
MIB = 1024 * 1024

epsilon = 1e-06
theta = 10000.0
masked = -1e30


def place(x, y, core):
    return (x * SIDE + y) * 2 + core


def step_pairs(dx, dy, flip=0):
    pairs = []
    for x in range(SIDE):
        for y in range(SIDE):
            for core in range(2):
                there = place((x + dx) % SIDE, (y + dy) % SIDE, core ^ flip)
                pairs.append((place(x, y, core), there))
    return pairs


def along_x(value, step):
    return lax.ppermute(value, "expert", step_pairs(step, 0))


def along_y(value, step):
    return lax.ppermute(value, "expert", step_pairs(0, step))


def along_z(value, step):
    return lax.ppermute(value, "dp", [(i, (i + step) % SIDE) for i in range(SIDE)])


def swap_core(value):
    return lax.ppermute(value, "expert", step_pairs(0, 0, 1))


def plane_groups():
    return [[2 * chip + core for chip in range(SIDE * SIDE)] for core in range(2)]


def tied(*values):
    return lax.optimization_barrier(values)


def ring_start(parts, move):
    half = parts.shape[1] // 2
    return move(parts[2, :half], 1), move(parts[2, half:], -1)


def ring_operands(parts, first):
    half = parts.shape[1] // 2
    ahead, behind = first
    up = jnp.concatenate([parts[1, :half] + ahead, parts[1, half:]], axis=0)
    down = jnp.concatenate([parts[3, :half], parts[3, half:] + behind], axis=0)
    return up, down


def ring_end(parts, second):
    return parts[0].astype(F32) + second[0].astype(F32) + second[1].astype(F32)


def low(parts):
    return parts.astype(BF)


def block_at(whole, index, rows):
    return lax.dynamic_slice_in_dim(whole, (index % SIDE) * rows, rows, axis=0)


def scatter_sum(whole, tail, here, move):
    rows = whole.shape[0] // SIDE
    total = jnp.concatenate([block_at(whole, here, rows), tail], axis=0).astype(F32)
    for r, step in ((1, 1), (2, 2), (3, -1)):
        send = jnp.concatenate([block_at(whole, here + r, rows), tail], axis=0)
        total = total + move(send, step).astype(F32)
    total = total.astype(BF)
    return total[:rows], total[rows:]


def ring_pieces(part, move):
    return [part, move(part, -1), move(part, 2), move(part, 1)]


def nt(a, b):
    return lax.dot_general(a, b, (((1,), (1,)), ((), ())), preferred_element_type=F32)


def tn(a, b):
    return lax.dot_general(a, b, (((0,), (0,)), ((), ())), preferred_element_type=F32)


def nn(a, b):
    return jnp.dot(a, b, preferred_element_type=F32)


def head_mean(values, head):
    n = values.shape[1]
    same = lax.broadcasted_iota(jnp.int32, (n, n), 0) // head == (
        lax.broadcasted_iota(jnp.int32, (n, n), 1) // head
    )
    ones = jnp.where(same, 1.0, 0.0).astype(BF)
    high = values.astype(BF)
    rest = values - high.astype(F32)
    middle = rest.astype(BF)
    low = (rest - middle.astype(F32)).astype(BF)
    return (nn(high, ones) + nn(middle, ones) + nn(low, ones)) * (1.0 / head)


def turn(values, cosine, sine, head):
    half = head // 2
    pieces = []
    lane = lax.broadcasted_iota(jnp.int32, (values.shape[0], 128), 1) % head
    for at in range(0, values.shape[1], 128):
        piece = values[:, at : at + 128]
        other = jnp.where(
            lane < half, pltpu.roll(piece, 128 - half, 1), pltpu.roll(piece, half, 1)
        )
        pieces.append(piece * cosine + other * sine)
    return pieces[0] if len(pieces) == 1 else jnp.concatenate(pieces, axis=1)


def allowed_keys(start, block, rows):
    length = (block + 1) * rows
    key = lax.broadcasted_iota(jnp.int32, (rows, length), 1)
    query = lax.broadcasted_iota(jnp.int32, (rows, length), 0) + block * rows
    return (key <= query) & (key >= start)


def attend_kernel(
    at_ref,
    x0_ref,
    x1_ref,
    x2_ref,
    x3_ref,
    gain_ref,
    wq_ref,
    wk_ref,
    wv_ref,
    qgain_ref,
    kgain_ref,
    cos_ref,
    sin_ref,
    start_ref,
    normed_ref,
    q_ref,
    k_ref,
    v_ref,
    qraw_ref,
    kraw_ref,
    out_ref,
    head,
):
    z = at_ref[0]
    rows = x0_ref.shape[0]
    for r, x_ref in enumerate((x0_ref, x1_ref, x2_ref, x3_ref)):
        here = pl.ds(pl.multiple_of(lax.rem(z - r + SIDE, SIDE) * rows, rows), rows)
        x = x_ref[...].astype(F32)
        scale = lax.rsqrt(jnp.mean(x * x, axis=-1, keepdims=True) + epsilon)
        normed = (x * scale * gain_ref[...]).astype(BF)
        normed_ref[here] = normed
        cosine, sine = cos_ref[here], sin_ref[here]
        q_raw = nn(normed, wq_ref[...])
        k_raw = nn(normed, wk_ref[...])
        v_ref[here] = nn(normed, wv_ref[...]).astype(BF)
        qraw_ref[here] = q_raw
        kraw_ref[here] = k_raw
        q = q_raw * lax.rsqrt(head_mean(q_raw * q_raw, head) + epsilon) * qgain_ref[...]
        k = k_raw * lax.rsqrt(head_mean(k_raw * k_raw, head) + epsilon) * kgain_ref[...]
        q_ref[here] = turn(q, cosine, sine, head).astype(BF) * (head**-0.5)
        k_ref[here] = turn(k, cosine, sine, head).astype(BF)
    for i in range(SIDE):
        length = (i + 1) * rows
        keep = allowed_keys(start_ref[i * rows : (i + 1) * rows], i, rows)
        outs = []
        for h in range(q_ref.shape[1] // head):
            j = h // 2
            q = q_ref[i * rows : (i + 1) * rows, h * head : (h + 1) * head]
            k = k_ref[:length, j * head : (j + 1) * head]
            v = v_ref[:length, j * head : (j + 1) * head]
            expo = jnp.where(keep, jnp.exp(nt(q, k)), 0.0)
            total = jnp.sum(expo, axis=1, keepdims=True)
            outs.append(nn(expo.astype(BF), v) / total)
        out_ref[lax.rem(i - z + SIDE, SIDE)] = jnp.concatenate(outs, axis=1).astype(BF)


def attend(at, x_rel, gain, query_proj, key_proj, value_proj, qgain, kgain, cosine, sine, start):
    rows, width = x_rel[0].shape
    length = SIDE * rows
    head = qgain.shape[0]
    q_cols, k_cols = query_proj.shape[1] // SIDE, key_proj.shape[1] // SIDE

    def whole(shape):
        return pl.BlockSpec(shape, lambda g, at: (0,) * len(shape))

    def columns(cols):
        return pl.BlockSpec((width, cols), lambda g, at: (0, at[0]))

    shapes = [
        ((length, width), BF),
        ((length, q_cols), BF),
        ((length, k_cols), BF),
        ((length, k_cols), BF),
        ((length, q_cols), F32),
        ((length, k_cols), F32),
        ((SIDE, rows, q_cols), BF),
    ]

    def kernel(*refs):
        attend_kernel(*refs, head=head)

    return pl.pallas_call(
        kernel,
        grid_spec=pltpu.PrefetchScalarGridSpec(
            num_scalar_prefetch=1,
            grid=(1,),
            in_specs=[whole((rows, width))] * SIDE
            + [whole((1, width)), columns(q_cols), columns(k_cols), columns(k_cols)]
            + [whole((1, q_cols)), whole((1, k_cols))]
            + [whole((length, 128)), whole((length, 128)), whole((length, 1))],
            out_specs=[whole(shape) for shape, _ in shapes],
        ),
        out_shape=[jax.ShapeDtypeStruct(shape, dtype) for shape, dtype in shapes],
        compiler_params=pltpu.CompilerParams(vmem_limit_bytes=48 * MIB),
        cost_estimate=pl.CostEstimate(
            flops=6_000_000_000, bytes_accessed=12_000_000, transcendentals=4_000_000
        ),
        name="attend",
    )(
        at,
        *x_rel,
        gain[None],
        query_proj,
        key_proj,
        value_proj,
        jnp.tile(qgain, q_cols // head)[None],
        jnp.tile(kgain, k_cols // head)[None],
        cosine,
        sine,
        start,
    )


def norm_back(raw, upstream, gain, head):
    scale = lax.rsqrt(head_mean(raw * raw, head) + epsilon)
    gain_grad = jnp.sum(upstream * raw * scale, axis=0, keepdims=True)
    weighted = upstream * gain
    inner = head_mean(weighted * raw, head)
    return scale * weighted - raw * (scale * scale * scale) * inner, gain_grad


def attend_back_kernel(
    at_ref,
    d0_ref,
    d1_ref,
    d2_ref,
    d3_ref,
    q_ref,
    k_ref,
    v_ref,
    qraw_ref,
    kraw_ref,
    qgain_ref,
    kgain_ref,
    cos_ref,
    sin_ref,
    start_ref,
    dqkv_ref,
    gains_ref,
    do_scr,
    dk_scr,
    dv_scr,
    head,
):
    z = at_ref[0]
    rows = d0_ref.shape[0]
    q_cols, k_cols = q_ref.shape[1], k_ref.shape[1]
    for r, d_ref in enumerate((d0_ref, d1_ref, d2_ref, d3_ref)):
        here = pl.ds(pl.multiple_of(lax.rem(z - r + SIDE, SIDE) * rows, rows), rows)
        do_scr[here] = d_ref[...]
    gains_ref[...] = jnp.zeros_like(gains_ref)
    for i in reversed(range(SIDE)):
        length = (i + 1) * rows
        here = slice(i * rows, (i + 1) * rows)
        keep = allowed_keys(start_ref[here], i, rows)
        d_queries = []
        for j in range(k_cols // head):
            k = k_ref[:length, j * head : (j + 1) * head]
            v = v_ref[:length, j * head : (j + 1) * head]
            d_key, d_value = 0.0, 0.0
            for h in (2 * j, 2 * j + 1):
                q = q_ref[here, h * head : (h + 1) * head]
                grad = do_scr[here, h * head : (h + 1) * head]
                expo = jnp.where(keep, jnp.exp(nt(q, k)), 0.0)
                probs = expo * (1.0 / jnp.sum(expo, axis=1, keepdims=True))
                d_probs = nt(grad, v)
                inner = jnp.sum(probs * d_probs, axis=1, keepdims=True)
                d_scores = (probs * (d_probs - inner)).astype(BF)
                d_queries.append(nn(d_scores, k) * (head**-0.5))
                d_key = d_key + tn(d_scores, q)
                d_value = d_value + tn(probs.astype(BF), grad)
            if i == SIDE - 1:
                dk_scr[j] = d_key
                dv_scr[j] = d_value
            else:
                dk_scr[j, :length] += d_key
                dv_scr[j, :length] += d_value
        d_query = jnp.concatenate(d_queries, axis=1)
        d_query = turn(d_query, cos_ref[here], -sin_ref[here], head)
        d_raw, d_gain = norm_back(qraw_ref[here], d_query, qgain_ref[...], head)
        dqkv_ref[here, :q_cols] = d_raw.astype(BF)
        gains_ref[0:1] += d_gain
        d_key = jnp.concatenate([dk_scr[0, here], dk_scr[1, here]], axis=1)
        d_key = turn(d_key, cos_ref[here], -sin_ref[here], head)
        d_raw, d_gain = norm_back(kraw_ref[here], d_key, kgain_ref[...], head)
        dqkv_ref[here, q_cols : q_cols + k_cols] = d_raw.astype(BF)
        gains_ref[1:2, :k_cols] += d_gain
        d_value = jnp.concatenate([dv_scr[0, here], dv_scr[1, here]], axis=1)
        dqkv_ref[here, q_cols + k_cols :] = d_value.astype(BF)


def attend_back(at, d_rel, q, k, v, q_raw, k_raw, qgain, kgain, cosine, sine, start):
    rows = d_rel[0].shape[0]
    length, q_cols = q.shape
    k_cols = k.shape[1]
    head = qgain.shape[0]

    def whole(shape):
        return pl.BlockSpec(shape, lambda g, at: (0,) * len(shape))

    def kernel(*refs):
        attend_back_kernel(*refs, head=head)

    operands = [
        *d_rel,
        q,
        k,
        v,
        q_raw,
        k_raw,
        jnp.tile(qgain, q_cols // head)[None],
        jnp.tile(kgain, k_cols // head)[None],
        cosine,
        sine,
        start,
    ]
    shapes = [((length, q_cols + 2 * k_cols), BF), ((8, q_cols), F32)]
    return pl.pallas_call(
        kernel,
        grid_spec=pltpu.PrefetchScalarGridSpec(
            num_scalar_prefetch=1,
            grid=(1,),
            in_specs=[whole(a.shape) for a in operands],
            out_specs=[whole(shape) for shape, _ in shapes],
            scratch_shapes=[
                pltpu.VMEM((length, q_cols), BF),
                pltpu.VMEM((k_cols // head, length, head), F32),
                pltpu.VMEM((k_cols // head, length, head), F32),
            ],
        ),
        out_shape=[jax.ShapeDtypeStruct(shape, dtype) for shape, dtype in shapes],
        compiler_params=pltpu.CompilerParams(vmem_limit_bytes=48 * MIB),
        cost_estimate=pl.CostEstimate(
            flops=8_000_000_000, bytes_accessed=8_000_000, transcendentals=4_000_000
        ),
        name="attend_back",
    )(at, *operands)


def expert_lines(routes, experts):
    line = lax.broadcasted_iota(jnp.int32, (experts, routes.shape[1]), 0).astype(F32)
    chosen = line == routes[0:1]
    for k in range(1, TOP):
        chosen = chosen | (line == routes[k : k + 1])
    return line, chosen


def pick_kernel(at_ref, cot_ref, down_ref, pick_ref, up_ref, dh_ref):
    tokens = pick_ref.shape[2]
    pick_iota = lax.broadcasted_iota(jnp.int32, (CAP, tokens), 0).astype(F32)
    tri = (
        lax.broadcasted_iota(jnp.int32, (tokens, tokens), 0)
        <= lax.broadcasted_iota(jnp.int32, (tokens, tokens), 1)
    ).astype(BF)
    mine = [at_ref[4 + j].astype(F32) for j in range(2)]
    members = []
    for s in range(SIDE):
        routes = cot_ref[0, s, tokens : tokens + 16, :tokens].astype(F32)
        for j in range(2):
            found = jnp.where(routes == mine[j], 1.0, 0.0)
            members.append(jnp.sum(found, axis=0, keepdims=True))
    member_all = jnp.concatenate(members, axis=0)
    rank_all = nn(member_all.astype(BF), tri)
    rank_all = jnp.where(member_all > 0.5, rank_all - 1.0, -1.0)
    for s in range(SIDE):
        for j in range(2):
            hit = pick_iota == rank_all[s * 2 + j : s * 2 + j + 1]
            pick_ref[s, j * CAP : (j + 1) * CAP] = jnp.where(hit, 1.0, 0.0).astype(BF)
        took = nn(pick_ref[s], cot_ref[0, s, :tokens]).astype(BF)
        for j in range(2):
            up_ref[j, s * CAP : (s + 1) * CAP] = took[j * CAP : (j + 1) * CAP]
    for j in range(2):
        dh_ref[j] = nt(up_ref[j], down_ref[j])


def moe_kernel(
    at_ref,
    rows_ref,
    routes_ref,
    pick_ref,
    dh_ref,
    router_ref,
    gate_ref,
    up_ref,
    back_a_ref,
    back_b_ref,
    x_ref,
    dgate_ref,
    dup_ref,
    hidden_ref,
    scaled_ref,
    share_ref,
    dgs_scr,
    b_scr,
):
    tokens = rows_ref.shape[2]
    half = rows_ref.shape[3] // 2
    y_here, chip = at_ref[2], at_ref[3]
    chip_row = lax.broadcasted_iota(jnp.int32, (SIDE * SIDE, half), 0) == chip
    mine = [at_ref[4 + j].astype(F32) for j in range(2)]
    for s in range(SIDE):
        rows = rows_ref[0, s]
        routes = routes_ref[0, s, :, :tokens].astype(F32)
        logits = nt(router_ref[...], rows)
        line, chosen = expert_lines(routes, router_ref.shape[0])
        top = jnp.max(jnp.where(chosen, logits, masked), axis=0, keepdims=True)
        expo = jnp.where(chosen, jnp.exp(jnp.minimum(logits - top, 0.0)), 0.0)
        share = expo / jnp.sum(expo, axis=0, keepdims=True)
        took = nn(pick_ref[s], rows).astype(BF)
        for j in range(2):
            own = jnp.sum(jnp.where(line == mine[j], share, 0.0), axis=0, keepdims=True)
            here = slice(s * CAP, (s + 1) * CAP)
            there = slice(j * CAP, (j + 1) * CAP)
            share_ref[j, here] = jnp.sum(
                pick_ref[s, there].astype(F32) * own, axis=1, keepdims=True
            )
            x_ref[j, here] = took[there]
    for j in range(2):
        x = x_ref[j]
        gate_act = nn(x, gate_ref[j])
        up_act = nn(x, up_ref[j])
        sig = 1.0 / (1.0 + jnp.exp(-gate_act))
        silu = gate_act * sig
        hidden = (silu * up_act).astype(BF)
        hidden_ref[j] = hidden
        scaled_ref[j] = (hidden.astype(F32) * share_ref[j]).astype(BF)
        raw = dh_ref[j]
        dgs_scr[j] = jnp.sum(hidden.astype(F32) * raw, axis=1, keepdims=True)
        d_hidden = raw * share_ref[j]
        d_gate = (d_hidden * up_act * (sig + silu * (1.0 - sig))).astype(BF)
        d_up = (d_hidden * silu).astype(BF)
        dgate_ref[j] = d_gate
        dup_ref[j] = d_up
        d_rows = (nt(d_gate, gate_ref[j]) + nt(d_up, up_ref[j])).astype(BF)
        for s in range(SIDE):
            b_scr[s, j * CAP : (j + 1) * CAP] = d_rows[s * CAP : (s + 1) * CAP]
    for s in range(SIDE):
        dy = lax.rem(s - y_here + SIDE, SIDE)
        back = tn(pick_ref[s], b_scr[s]).astype(BF)
        back_a_ref[0, dy, :tokens] = back[:, :half]
        back_b_ref[dy, 0, :tokens] = back[:, half:]
        found = []
        for j in range(2):
            col = dgs_scr[j, s * CAP : (s + 1) * CAP]
            pick = pick_ref[s, j * CAP : (j + 1) * CAP].astype(F32)
            found.append(jnp.sum(pick * col, axis=0, keepdims=True))
        found = jnp.where(chip_row, jnp.concatenate(found, axis=1), 0.0)
        high = found.astype(BF)
        back_a_ref[0, dy, tokens:] = high
        back_b_ref[dy, 0, tokens:] = (found - high.astype(F32)).astype(BF)


def result_kernel(at_ref, hidden_ref, share_ref, pick_ref, down_ref, out_ref, o_scr):
    for j in range(2):
        share = share_ref[j]
        result = nn(hidden_ref[j], down_ref[j]).astype(BF).astype(F32)
        gated = (share * result).astype(BF)
        for s in range(SIDE):
            o_scr[s, j * CAP : (j + 1) * CAP] = gated[s * CAP : (s + 1) * CAP]
    for s in range(SIDE):
        out_ref[0, s] = tn(pick_ref[s], o_scr[s]).astype(BF)


def over_sources(kernel, at, operands, outs, scratch, flops, name):
    return pl.pallas_call(
        kernel,
        grid_spec=pltpu.PrefetchScalarGridSpec(
            num_scalar_prefetch=1,
            grid=(SIDE,),
            in_specs=[pl.BlockSpec(block, index) for _, block, index in operands],
            out_specs=[pl.BlockSpec(block, index) for _, block, index in outs],
            scratch_shapes=scratch,
        ),
        out_shape=[jax.ShapeDtypeStruct(*what) for what, _, _ in outs],
        compiler_params=pltpu.CompilerParams(vmem_limit_bytes=60 * MIB),
        cost_estimate=pl.CostEstimate(flops=flops, bytes_accessed=30_000_000, transcendentals=0),
        name=name,
    )(at, *[array for array, _, _ in operands])


def source(g, at):
    return (at[1] + 2 + g) % SIDE


def by_source(rank, axis):
    return lambda g, at: tuple(source(g, at) if n == axis else 0 for n in range(rank))


def fixed(array):
    return array, array.shape, lambda g, at: (0,) * array.ndim


def moe_before(at, cot, down):
    _, _, padded, width = cot.shape
    tokens, slots, ff = padded - 16, SIDE * CAP, down.shape[1]
    return over_sources(
        pick_kernel,
        at,
        [(cot, (1, SIDE, padded, width), by_source(4, 0)), fixed(down)],
        [
            (((SIDE * SIDE, 2 * CAP, tokens), BF), (SIDE, 2 * CAP, tokens), by_source(3, 0)),
            (((2, SIDE * slots, width), BF), (2, slots, width), by_source(3, 1)),
            (((2, SIDE * slots, ff), F32), (2, slots, ff), by_source(3, 1)),
        ],
        [],
        4_000_000_000,
        "moe_before",
    )


def moe(at, rows, cot, pick, raw, router_t, gate, up):
    _, _, tokens, width = rows.shape
    padded = cot.shape[2]
    ff, slots, half = gate.shape[2], SIDE * CAP, width // 2

    def first(g, at):
        return ((2 + g) % SIDE, 0, 0, 0)

    def second(g, at):
        return (0, (2 + g) % SIDE, 0, 0)

    def kept(cols, dtype):
        return ((2, SIDE * slots, cols), dtype), (2, slots, cols), by_source(3, 1)

    return over_sources(
        moe_kernel,
        at,
        [
            (rows, (1, SIDE, tokens, width), by_source(4, 0)),
            (cot, (1, SIDE, 16, width), lambda g, at: (source(g, at), 0, tokens // 16, 0)),
            (pick, (SIDE, 2 * CAP, tokens), by_source(3, 0)),
            (raw, (2, slots, ff), by_source(3, 1)),
            fixed(router_t),
            fixed(gate),
            fixed(up),
        ],
        [
            (((SIDE, SIDE, padded, half), BF), (1, SIDE, padded, half), first),
            (((SIDE, SIDE, padded, half), BF), (SIDE, 1, padded, half), second),
            kept(width, BF),
            kept(ff, BF),
            kept(ff, BF),
            kept(ff, BF),
            kept(ff, BF),
            kept(1, F32),
        ],
        [pltpu.VMEM((2, slots, 1), F32), pltpu.VMEM((SIDE, 2 * CAP, width), BF)],
        14_000_000_000,
        "moe",
    )


def moe_result(at, hidden, share, pick, down):
    slots, ff, width = SIDE * CAP, hidden.shape[2], down.shape[2]
    tokens = pick.shape[2]

    def part(array):
        return array, (2, slots, array.shape[2]), by_source(3, 1)

    return over_sources(
        result_kernel,
        at,
        [part(hidden), part(share)]
        + [(pick, (SIDE, 2 * CAP, tokens), by_source(3, 0)), fixed(down)],
        [
            (((SIDE, SIDE, tokens, width), BF), (1, SIDE, tokens, width), by_source(4, 0)),
        ],
        [pltpu.VMEM((SIDE, 2 * CAP, width), BF)],
        4_000_000_000,
        "moe_result",
    )[0]


def middle_kernel(at_ref, a0_ref, a1_ref, a2_ref, a3_ref, x_ref, w_ref, gain_ref, mid_ref, low_ref):
    z = at_ref[0]
    cols = a0_ref.shape[1]
    total = x_ref[...].astype(F32)
    for r, a_ref in enumerate((a0_ref, a1_ref, a2_ref, a3_ref)):
        there = pl.ds(pl.multiple_of(lax.rem(z - r + SIDE, SIDE) * cols, cols), cols)
        total = total + nn(a_ref[...], w_ref[there])
    mid_ref[...] = total
    scale = lax.rsqrt(jnp.mean(total * total, axis=-1, keepdims=True) + epsilon)
    low_ref[...] = (total * scale * gain_ref[...]).astype(BF)


def in_vmem(kernel, at, operands, shapes, scratch, flops, name):
    def whole(shape):
        return pl.BlockSpec(shape, lambda g, at: (0,) * len(shape))

    return pl.pallas_call(
        kernel,
        grid_spec=pltpu.PrefetchScalarGridSpec(
            num_scalar_prefetch=1,
            grid=(1,),
            in_specs=[whole(a.shape) for a in operands],
            out_specs=[whole(shape) for shape, _ in shapes],
            scratch_shapes=scratch,
        ),
        out_shape=[jax.ShapeDtypeStruct(shape, dtype) for shape, dtype in shapes],
        compiler_params=pltpu.CompilerParams(vmem_limit_bytes=56 * MIB),
        cost_estimate=pl.CostEstimate(flops=flops, bytes_accessed=8_000_000, transcendentals=0),
        name=name,
    )(at, *operands)


def post_kernel(
    at_ref,
    a0_ref,
    a1_ref,
    a2_ref,
    b0_ref,
    b1_ref,
    b2_ref,
    mid_ref,
    low_ref,
    gain_ref,
    router_ref,
    routes_ref,
    cot_ref,
    w_ref,
    d_mid_ref,
    branch_ref,
    att0_ref,
    att1_ref,
    att2_ref,
    att3_ref,
    router_grad_ref,
    gain_grad_ref,
):
    z, core = at_ref[0], at_ref[6]
    tokens = mid_ref.shape[0]
    chips = SIDE * SIDE
    cols = att0_ref.shape[1]
    side_a = a0_ref[...].astype(F32) + a1_ref[...].astype(F32) + a2_ref[...].astype(F32)
    side_b = b0_ref[...].astype(F32) + b1_ref[...].astype(F32) + b2_ref[...].astype(F32)
    found = side_a[tokens:] + side_b[tokens:]
    d_gates = jnp.concatenate([found[:, :tokens], found[:, tokens:]], axis=0)
    line = lax.broadcasted_iota(jnp.int32, (2 * chips, tokens), 0)
    second = line >= chips
    expert = 2 * jnp.where(second, line - chips, line) + jnp.where(second, 1 - core, core)
    expert = expert.astype(F32)
    routes = routes_ref[...].astype(F32)
    chosen = expert == routes[0:1]
    for k in range(1, TOP):
        chosen = chosen | (expert == routes[k : k + 1])
    logits = nt(router_ref[...], low_ref[...])
    top = jnp.max(jnp.where(chosen, logits, masked), axis=0, keepdims=True)
    expo = jnp.where(chosen, jnp.exp(jnp.minimum(logits - top, 0.0)), 0.0)
    share = expo / jnp.sum(expo, axis=0, keepdims=True)
    d_gates = jnp.where(chosen, d_gates, 0.0)
    d_logits = share * (d_gates - jnp.sum(share * d_gates, axis=0, keepdims=True))
    d_logits = d_logits.astype(BF)
    router_grad_ref[...] = nn(d_logits, low_ref[...])
    d_normed = jnp.concatenate([side_a[:tokens], side_b[:tokens]], axis=1)
    d_normed = d_normed + tn(d_logits, router_ref[...])
    mid = mid_ref[...]
    scale = lax.rsqrt(jnp.mean(mid * mid, axis=-1, keepdims=True) + epsilon)
    gain_grad_ref[...] = jnp.sum(d_normed * mid * scale, axis=0, keepdims=True)
    weighted = d_normed * gain_ref[...]
    inner = jnp.mean(weighted * mid, axis=-1, keepdims=True)
    d_mid = cot_ref[...].astype(F32) + scale * weighted - mid * (scale * scale * scale) * inner
    d_mid_ref[...] = d_mid
    branch = d_mid.astype(BF)
    branch_ref[...] = branch
    for r, att_ref in enumerate((att0_ref, att1_ref, att2_ref, att3_ref)):
        there = pl.ds(pl.multiple_of(lax.rem(z + r, SIDE) * cols, cols), cols)
        att_ref[...] = nt(branch, w_ref[there]).astype(BF)


def weights_kernel(at_ref, normed_ref, dqkv_ref, att_ref, b0_ref, b1_ref, b2_ref, b3_ref, out_ref):
    cols = dqkv_ref.shape[1]
    rows, heads = att_ref.shape[1:]
    out_ref[:, :cols] = tn(normed_ref[...], dqkv_ref[...]).astype(BF)
    total = None
    for r, b_ref in enumerate((b0_ref, b1_ref, b2_ref, b3_ref)):
        part = tn(att_ref[(SIDE - r) % SIDE], b_ref[...])
        total = part if total is None else total + part
    total = total.astype(BF)
    for n in range(total.shape[1] // heads):
        out_ref[n * heads : (n + 1) * heads, cols:] = total[:, n * heads : (n + 1) * heads]


def finish_kernel(at_ref, *refs):
    pieces, (wq_ref, wk_ref, wv_ref, gain_ref) = refs[:16], refs[16:20]
    q_ref, k_ref, v_ref, o_ref, gain_grad_ref = refs[20:]
    z, x_at, y_at, core = at_ref[0], at_ref[1], at_ref[2], at_ref[6]
    width = q_ref.shape[0]
    heads, kv = width // SIDE, k_ref.shape[1] // SIDE
    rows = width // (2 * SIDE * SIDE)
    for own in range(2):
        base = jnp.where(core == own, 0, width // 2)
        for side in range(2):
            for far in range(SIDE):
                ref = pieces[own * 8 + side * 4 + far]

                for near in range(SIDE):
                    rx, ry = (far, near) if side == 0 else (near, far)
                    xs, ys = lax.rem(x_at + rx, SIDE), lax.rem(y_at + ry, SIDE)
                    row = pl.multiple_of(base + (xs * SIDE + ys) * rows, rows)
                    here = pl.ds(row, rows)
                    group = lax.div(row, heads)
                    inside = row - group * heads
                    at_o = pl.ds(pl.multiple_of(group * heads, heads), heads)
                    for rz in range(SIDE):
                        zs = lax.rem(z + rz, SIDE)
                        block = ref[near, rz].astype(F32)
                        at_q = pl.ds(pl.multiple_of(zs * heads, heads), heads)
                        at_k = pl.ds(pl.multiple_of(zs * kv, kv), kv)
                        if side == 0:
                            q_ref[here, at_q] = block[:, :heads]
                            k_ref[here, at_k] = block[:, heads:]
                        else:
                            v_ref[here, at_k] = block[:, :kv]
                            o_row = pl.multiple_of(zs * heads + inside, rows)
                            o_ref[pl.ds(o_row, rows), at_o] = block[:, kv:]
    for n in range(SIDE):
        here = slice(n * heads, (n + 1) * heads)
        total = jnp.sum(q_ref[here] * wq_ref[here].astype(F32), axis=1, keepdims=True)
        total = total + jnp.sum(k_ref[here] * wk_ref[here].astype(F32), axis=1, keepdims=True)
        total = total + jnp.sum(v_ref[here] * wv_ref[here].astype(F32), axis=1, keepdims=True)
        gain_grad_ref[here] = total / gain_ref[here]


def rms_back(values, scale, gain, upstream):
    weighted = upstream * gain
    inner = jnp.mean(weighted * values, axis=-1, keepdims=True)
    return scale * weighted - values * (scale * scale * scale) * inner


def body(
    block_input,
    attn_norm_gain,
    query_proj,
    key_proj,
    value_proj,
    query_gain,
    key_gain,
    output_proj,
    ffn_norm_gain,
    router_proj,
    expert_routes,
    document_ids,
    expert_gate,
    expert_up,
    expert_down,
    cotangent,
):
    tokens, width = block_input.shape[1:]
    head = query_gain.shape[0]
    experts_all = router_proj.shape[1]
    z = lax.axis_index("dp")
    expert_at = lax.axis_index("expert")
    chip, core = expert_at // 2, expert_at % 2
    x_at, y_at = chip // SIDE, chip % SIDE
    at = jnp.stack([z, x_at, y_at, chip, expert_at, expert_at + 1 - 2 * core, core])
    at = at.astype(jnp.int32)

    own = block_input[0]
    route_rows = jnp.full((16, width), -1.0, BF)
    route_rows = lax.dynamic_update_slice(route_rows, expert_routes[0].T.astype(BF), (0, 0))
    cot_rows = jnp.concatenate([cotangent[0], route_rows], axis=0)
    own, cot_rows = tied(own, cot_rows)
    cot_all = lax.all_gather(cot_rows, "expert", axis_index_groups=plane_groups())
    x_rel = [own, along_z(own, 1), along_z(own, 2), along_z(own, -1)]

    doc = document_ids[0]
    below_one = jnp.sum((doc < 1).astype(jnp.int32))
    below_two = jnp.sum((doc < 2).astype(jnp.int32))
    start = jnp.where(doc < 1, 0, jnp.where(doc < 2, below_one, below_two)).astype(jnp.int32)
    position = (jnp.arange(doc.shape[0], dtype=jnp.int32) - start).astype(F32)
    frequency = theta ** (-jnp.arange(head // 2, dtype=F32) * 2.0 / head)
    angles = position[:, None] * frequency[None, :]
    cosine, sine = jnp.cos(angles), jnp.sin(angles)
    cosine = jnp.tile(cosine, (1, 4))
    sine = jnp.tile(jnp.concatenate([-sine, sine], axis=1), (1, 2))
    start = start[:, None]

    normed_all, q, k, v, q_raw, k_raw, out_rel = attend(
        at,
        x_rel,
        attn_norm_gain,
        query_proj,
        key_proj,
        value_proj,
        query_gain,
        key_gain,
        cosine,
        sine,
        start,
    )
    q_cols, k_cols = q.shape[1], k.shape[1]

    att_rel = [out_rel[0]] + [along_z(out_rel[r], t) for r, t in ((1, 1), (2, 2), (3, -1))]
    middle, normed_two = in_vmem(
        middle_kernel,
        at,
        [*att_rel, own, output_proj, ffn_norm_gain[None]],
        [((tokens, width), F32), ((tokens, width), BF)],
        [],
        600_000_000,
        "middle",
    )
    normed_two, cot_all = tied(normed_two, cot_all)
    rows_all = lax.all_gather(normed_two, "expert", axis_index_groups=plane_groups())
    gate_two = jnp.concatenate([expert_gate, swap_core(expert_gate)], axis=0)
    up_two = jnp.concatenate([expert_up, swap_core(expert_up)], axis=0)
    down_two = jnp.concatenate([expert_down, swap_core(expert_down)], axis=0)
    cot_all = cot_all.reshape(SIDE, SIDE, tokens + 16, width)
    pick, upstream, raw = moe_before(at, cot_all, down_two)
    back_a, back_b, kept_x, kept_dg, kept_du, kept_h, kept_s, share = moe(
        at,
        rows_all.reshape(SIDE, SIDE, tokens, width),
        cot_all,
        pick,
        raw,
        router_proj.T,
        gate_two,
        up_two,
    )
    out = moe_result(at, kept_h, share, pick, down_two)

    def slots_grad(a, b):
        return jnp.einsum("jrd,jrf->jdf", a, b, preferred_element_type=F32).astype(BF)

    first_a, first_b = ring_start(back_a, along_x), ring_start(back_b, along_y)
    gate_w = slots_grad(kept_x, kept_dg)
    up_a, down_a = ring_operands(back_a, first_a)
    up_b, down_b = ring_operands(back_b, first_b)
    up_a, down_a, up_b, down_b = tied(up_a, down_a, up_b, down_b)
    second_a = along_x(up_a, 1), along_x(down_a, -1)
    second_b = along_y(up_b, 1), along_y(down_b, -1)
    up_w = slots_grad(kept_x, kept_du)
    down_w = slots_grad(upstream, kept_s)
    second_a, second_b, gate_w, up_w, down_w, out = tied(
        second_a, second_b, gate_w, up_w, down_w, out
    )
    whole_w = jnp.stack([gate_w, up_w, down_w], axis=1)
    whole_w = (whole_w[0].astype(F32) + swap_core(whole_w[1]).astype(F32)).astype(BF)
    expert_sum = lax.psum_scatter(whole_w, "dp", scatter_dimension=1, tiled=True)
    part_a, part_b = low(ring_end(back_a, second_a)), low(ring_end(back_b, second_b))
    part_a, part_b = tied(part_a, part_b)
    first_a, first_b = ring_start(part_a, along_y), ring_start(part_b, along_x)
    up_a, down_a = ring_operands(part_a, first_a)
    up_b, down_b = ring_operands(part_b, first_b)
    up_a, down_a, up_b, down_b = tied(up_a, down_a, up_b, down_b)
    second_a = along_y(up_a, 1), along_y(down_a, -1)
    second_b = along_x(up_b, 1), along_x(down_b, -1)

    chips = SIDE * SIDE
    router_two = router_proj.T.reshape(chips, 2, width)
    router_two = jnp.where(core == 0, router_two, router_two[:, ::-1])
    router_two = router_two.transpose(1, 0, 2).reshape(experts_all, width)
    d_middle, d_branch, *d_att, router_local, ffn_gain_local = in_vmem(
        post_kernel,
        at,
        [part_a[0], *second_a, part_b[0], *second_b, middle, normed_two, ffn_norm_gain[None]]
        + [router_two, route_rows[:, :tokens], cotangent[0], output_proj],
        [
            ((tokens, width), F32),
            ((tokens, width), BF),
            *[((tokens, q_cols), BF)] * SIDE,
            ((experts_all, width), F32),
            ((1, width), F32),
        ],
        [],
        600_000_000,
        "post",
    )

    *d_att, out = tied(*d_att, out)
    d_rel = [d_att[0]] + [along_z(d_att[r], t) for r, t in ((1, 1), (2, 2), (3, -1))]
    out = lax.psum_scatter(
        out.reshape(chips * tokens, width),
        "expert",
        axis_index_groups=plane_groups(),
        scatter_dimension=0,
        tiled=True,
    )
    d_rel[1], d_branch_sent = tied(d_rel[1], d_branch)
    branch_rel = [d_branch] + [along_z(d_branch_sent, t) for t in (1, 2, -1)]
    router_local = jnp.where(core == 0, router_local, jnp.roll(router_local, chips, axis=0))
    few = jnp.concatenate([router_local, ffn_gain_local], axis=0)
    few = jnp.concatenate([few, jnp.zeros((15, width), F32)], axis=0).astype(BF)
    few, d_rel[2] = tied(few, d_rel[2])
    few = few.astype(F32) + sum(along_z(few, t).astype(F32) for t in (1, 2, -1))
    few = lax.dynamic_slice_in_dim(few[: experts_all + 1], z * q_cols, q_cols, axis=1)
    few = few.reshape(-1, 3 * q_cols)
    few = jnp.pad(few, ((0, 16 - few.shape[0]), (0, 0))).astype(BF)
    dqkv, gains = attend_back(
        at, d_rel, q, k, v, q_raw, k_raw, query_gain, key_gain, cosine, sine, start
    )

    local = in_vmem(
        weights_kernel,
        at,
        [normed_all, dqkv, out_rel, *branch_rel],
        [((width, 2 * q_cols + 2 * k_cols), BF)],
        [],
        1_600_000_000,
        "weights",
    )[0]
    tail = jnp.concatenate([gains[0], gains[1], jnp.zeros_like(gains[0])])
    tail = jnp.pad(tail[None], ((0, 15), (0, 0))).astype(BF)
    tail = jnp.concatenate([tail, few], axis=0)
    half = width // 2
    mine = lax.dynamic_slice_in_dim(local, core * half, half, axis=0)
    other = lax.dynamic_slice_in_dim(local, (1 - core) * half, half, axis=0)
    got = swap_core(jnp.concatenate([other, tail], axis=0)).astype(F32)
    part = (mine.astype(F32) + got[:half]).astype(BF)
    tail = (tail.astype(F32) + got[half:]).astype(BF)
    part, tail = scatter_sum(part, tail, x_at, along_x)
    part, tail = scatter_sum(part, tail, y_at, along_y)
    pieces = jnp.stack(ring_pieces(jnp.concatenate([part, tail], axis=0), along_z))
    rows = part.shape[0]
    gain_sums = jnp.sum(pieces[:, rows].astype(F32), axis=0)
    few = pieces[:, rows + 16 : rows + 16 + (experts_all + 1) * q_cols // (3 * q_cols)]
    few = few.astype(F32).reshape(SIDE, experts_all + 1, q_cols)
    few = jnp.roll(few, z, axis=0).transpose(1, 0, 2).reshape(experts_all + 1, width)
    router_sum = few[:experts_all].reshape(2, chips, width).transpose(2, 1, 0)
    router_sum = router_sum.reshape(width, experts_all)
    split = q_cols + k_cols
    side_a, side_b = pieces[:, :rows, :split], pieces[:, :rows, split:]
    side_a = jnp.stack(ring_pieces(side_a, along_y))
    side_b = jnp.stack(ring_pieces(side_b, along_x))
    ends = ring_pieces(side_a, along_x) + ring_pieces(side_b, along_y)
    ends = ends + [swap_core(piece) for piece in ends]
    query_sum, key_sum, value_sum, output_sum, attn_gain_sum = in_vmem(
        finish_kernel,
        at,
        [*ends, query_proj, key_proj, value_proj, attn_norm_gain[:, None]],
        [
            ((width, SIDE * q_cols), F32),
            ((width, SIDE * k_cols), F32),
            ((width, SIDE * k_cols), F32),
            ((SIDE * q_cols, width), F32),
            ((width, 1), F32),
        ],
        [],
        10_000_000,
        "finish",
    )
    query_gain_sum = jnp.sum(gain_sums[:q_cols].reshape(-1, head), axis=0)
    key_gain_sum = jnp.sum(gain_sums[q_cols : q_cols + k_cols].reshape(-1, head), axis=0)

    expert_sum = expert_sum.astype(F32)
    gate_grad, up_grad = expert_sum[0:1], expert_sum[1:2]
    down_grad = jnp.transpose(expert_sum[2:3], (0, 2, 1))

    back = jnp.zeros((tokens, SIDE, q_cols + 2 * k_cols), BF)
    for r, step in ((0, 0), (1, 1), (2, 2), (3, -1)):
        piece = block_at(dqkv, z + r, tokens)
        piece = along_z(piece, step) if step else piece
        back = lax.dynamic_update_slice(back, piece[:, None], (0, (z - r) % SIDE, 0))
    d_query = back[:, :, :q_cols].reshape(tokens, -1)
    d_key = back[:, :, q_cols : q_cols + k_cols].reshape(tokens, -1)
    d_value = back[:, :, q_cols + k_cols :].reshape(tokens, -1)
    d_normed = nt(d_query, query_proj) + nt(d_key, key_proj) + nt(d_value, value_proj)
    inputs = own.astype(F32)
    scale_one = lax.rsqrt(jnp.mean(inputs * inputs, axis=-1, keepdims=True) + epsilon)
    input_grad = d_middle + rms_back(inputs, scale_one, attn_norm_gain, d_normed)

    block_output = (middle + out.astype(F32)).astype(BF)

    return (
        block_output[None],
        input_grad[None],
        attn_gain_sum[:, 0],
        query_sum,
        key_sum,
        value_sum,
        query_gain_sum,
        key_gain_sum,
        output_sum,
        few[experts_all],
        router_sum,
        gate_grad,
        up_grad,
        down_grad,
    )


def solution(mesh):
    tokens = P("expert", "dp", None)
    experts = P("expert", None, None)
    return jax.shard_map(
        body,
        mesh=mesh,
        in_specs=(tokens,)
        + (P(),) * 9
        + (tokens, P("expert", None), experts, experts, experts, tokens),
        out_specs=(tokens, tokens)
        + (P(),) * 9
        + (tokens, tokens, P("expert", None, "dp")),
        check_vma=False,
    )
```

```python
import jax
import jax.numpy as jnp
from jax import lax
from jax.experimental import pallas as pl
from jax.experimental.pallas import tpu as pltpu
from jax.sharding import PartitionSpec as P

CAP = 80
SIDE = 4
TOP = 8
BF = jnp.bfloat16
F32 = jnp.float32
MIB = 1024 * 1024

epsilon = 1e-06
theta = 10000.0
masked = -1e30


def place(x, y, core):
    return (x * SIDE + y) * 2 + core


def step_pairs(dx, dy, flip=0):
    pairs = []
    for x in range(SIDE):
        for y in range(SIDE):
            for core in range(2):
                there = place((x + dx) % SIDE, (y + dy) % SIDE, core ^ flip)
                pairs.append((place(x, y, core), there))
    return pairs


def along_x(value, step):
    return lax.ppermute(value, "expert", step_pairs(step, 0))


def along_y(value, step):
    return lax.ppermute(value, "expert", step_pairs(0, step))


def along_z(value, step):
    return lax.ppermute(value, "dp", [(i, (i + step) % SIDE) for i in range(SIDE)])


def swap_core(value):
    return lax.ppermute(value, "expert", step_pairs(0, 0, 1))


def plane_groups():
    return [[2 * chip + core for chip in range(SIDE * SIDE)] for core in range(2)]


def tied(*values):
    return lax.optimization_barrier(values)


def ring_start(parts, move):
    half = parts.shape[1] // 2
    return move(parts[2, :half], 1), move(parts[2, half:], -1)


def ring_operands(parts, first):
    half = parts.shape[1] // 2
    ahead, behind = first
    up = jnp.concatenate([parts[1, :half] + ahead, parts[1, half:]], axis=0)
    down = jnp.concatenate([parts[3, :half], parts[3, half:] + behind], axis=0)
    return up, down


def ring_end(parts, second):
    return parts[0].astype(F32) + second[0].astype(F32) + second[1].astype(F32)


def low(parts):
    return parts.astype(BF)


def block_at(whole, index, rows):
    return lax.dynamic_slice_in_dim(whole, (index % SIDE) * rows, rows, axis=0)


def scatter_sum(whole, tail, here, move):
    rows = whole.shape[0] // SIDE
    total = jnp.concatenate([block_at(whole, here, rows), tail], axis=0).astype(F32)
    for r, step in ((1, 1), (2, 2), (3, -1)):
        send = jnp.concatenate([block_at(whole, here + r, rows), tail], axis=0)
        total = total + move(send, step).astype(F32)
    total = total.astype(BF)
    return total[:rows], total[rows:]


def ring_pieces(part, move):
    return [part, move(part, -1), move(part, 2), move(part, 1)]


def nt(a, b):
    return lax.dot_general(a, b, (((1,), (1,)), ((), ())), preferred_element_type=F32)


def tn(a, b):
    return lax.dot_general(a, b, (((0,), (0,)), ((), ())), preferred_element_type=F32)


def nn(a, b):
    return jnp.dot(a, b, preferred_element_type=F32)


def head_mean(values, head):
    n = values.shape[1]
    same = lax.broadcasted_iota(jnp.int32, (n, n), 0) // head == (
        lax.broadcasted_iota(jnp.int32, (n, n), 1) // head
    )
    ones = jnp.where(same, 1.0, 0.0).astype(BF)
    high = values.astype(BF)
    rest = values - high.astype(F32)
    middle = rest.astype(BF)
    low = (rest - middle.astype(F32)).astype(BF)
    return (nn(high, ones) + nn(middle, ones) + nn(low, ones)) * (1.0 / head)


def turn(values, cosine, sine, head):
    half = head // 2
    pieces = []
    lane = lax.broadcasted_iota(jnp.int32, (values.shape[0], 128), 1) % head
    for at in range(0, values.shape[1], 128):
        piece = values[:, at : at + 128]
        other = jnp.where(
            lane < half, pltpu.roll(piece, 128 - half, 1), pltpu.roll(piece, half, 1)
        )
        pieces.append(piece * cosine + other * sine)
    return pieces[0] if len(pieces) == 1 else jnp.concatenate(pieces, axis=1)


def allowed_keys(start, block, rows):
    length = (block + 1) * rows
    key = lax.broadcasted_iota(jnp.int32, (rows, length), 1)
    query = lax.broadcasted_iota(jnp.int32, (rows, length), 0) + block * rows
    return (key <= query) & (key >= start)


def attend_kernel(
    at_ref,
    x0_ref,
    x1_ref,
    x2_ref,
    x3_ref,
    gain_ref,
    wq_ref,
    wk_ref,
    wv_ref,
    qgain_ref,
    kgain_ref,
    cos_ref,
    sin_ref,
    start_ref,
    normed_ref,
    q_ref,
    k_ref,
    v_ref,
    qraw_ref,
    kraw_ref,
    out_ref,
    p0_ref,
    p1_ref,
    p2_ref,
    p3_ref,
    head,
):
    z = at_ref[0]
    rows = x0_ref.shape[0]
    for r, x_ref in enumerate((x0_ref, x1_ref, x2_ref, x3_ref)):
        here = pl.ds(pl.multiple_of(lax.rem(z - r + SIDE, SIDE) * rows, rows), rows)
        x = x_ref[...].astype(F32)
        scale = lax.rsqrt(jnp.mean(x * x, axis=-1, keepdims=True) + epsilon)
        normed = x * scale * gain_ref[...]
        normed_ref[:, here] = normed.T.astype(BF)
        normed = normed.astype(BF)
        cosine, sine = cos_ref[here], sin_ref[here]
        q_raw = nn(normed, wq_ref[...])
        k_raw = nn(normed, wk_ref[...])
        v_ref[here] = nn(normed, wv_ref[...]).astype(BF)
        qraw_ref[here] = q_raw
        kraw_ref[here] = k_raw
        q = q_raw * lax.rsqrt(head_mean(q_raw * q_raw, head) + epsilon) * qgain_ref[...]
        k = k_raw * lax.rsqrt(head_mean(k_raw * k_raw, head) + epsilon) * kgain_ref[...]
        q_ref[here] = turn(q, cosine, sine, head).astype(BF) * (head**-0.5)
        k_ref[here] = turn(k, cosine, sine, head).astype(BF)
    for i, kept_ref in enumerate((p0_ref, p1_ref, p2_ref, p3_ref)):
        length = (i + 1) * rows
        keep = allowed_keys(start_ref[i * rows : (i + 1) * rows], i, rows)
        outs = []
        for h in range(q_ref.shape[1] // head):
            j = h // 2
            q = q_ref[i * rows : (i + 1) * rows, h * head : (h + 1) * head]
            k = k_ref[:length, j * head : (j + 1) * head]
            v = v_ref[:length, j * head : (j + 1) * head]
            expo = jnp.where(keep, jnp.exp(nt(q, k)), 0.0)
            total = jnp.sum(expo, axis=1, keepdims=True)
            probs = (expo * (1.0 / total)).astype(BF)
            kept_ref[h] = probs
            outs.append(nn(probs, v))
        out_ref[lax.rem(i - z + SIDE, SIDE)] = jnp.concatenate(outs, axis=1).astype(BF)


def attend(at, x_rel, gain, query_proj, key_proj, value_proj, qgain, kgain, cosine, sine, start):
    rows, width = x_rel[0].shape
    length = SIDE * rows
    head = qgain.shape[0]
    q_cols, k_cols = query_proj.shape[1] // SIDE, key_proj.shape[1] // SIDE

    def whole(shape):
        return pl.BlockSpec(shape, lambda g, at: (0,) * len(shape))

    def columns(cols):
        return pl.BlockSpec((width, cols), lambda g, at: (0, at[0]))

    shapes = [
        ((width, length), BF),
        ((length, q_cols), BF),
        ((length, k_cols), BF),
        ((length, k_cols), BF),
        ((length, q_cols), F32),
        ((length, k_cols), F32),
        ((SIDE, rows, q_cols), BF),
    ]
    shapes += [((q_cols // head, rows, (i + 1) * rows), BF) for i in range(SIDE)]

    def kernel(*refs):
        attend_kernel(*refs, head=head)

    return pl.pallas_call(
        kernel,
        grid_spec=pltpu.PrefetchScalarGridSpec(
            num_scalar_prefetch=1,
            grid=(1,),
            in_specs=[whole((rows, width))] * SIDE
            + [whole((1, width)), columns(q_cols), columns(k_cols), columns(k_cols)]
            + [whole((1, q_cols)), whole((1, k_cols))]
            + [whole((length, 128)), whole((length, 128)), whole((length, 1))],
            out_specs=[whole(shape) for shape, _ in shapes],
        ),
        out_shape=[jax.ShapeDtypeStruct(shape, dtype) for shape, dtype in shapes],
        compiler_params=pltpu.CompilerParams(vmem_limit_bytes=48 * MIB),
        cost_estimate=pl.CostEstimate(
            flops=6_000_000_000, bytes_accessed=12_000_000, transcendentals=4_000_000
        ),
        name="attend",
    )(
        at,
        *x_rel,
        gain[None],
        query_proj,
        key_proj,
        value_proj,
        jnp.tile(qgain, q_cols // head)[None],
        jnp.tile(kgain, k_cols // head)[None],
        cosine,
        sine,
        start,
    )


def norm_back(raw, upstream, gain, head):
    scale = lax.rsqrt(head_mean(raw * raw, head) + epsilon)
    gain_grad = jnp.sum(upstream * raw * scale, axis=0, keepdims=True)
    weighted = upstream * gain
    inner = head_mean(weighted * raw, head)
    return scale * weighted - raw * (scale * scale * scale) * inner, gain_grad


def attend_back_kernel(
    at_ref,
    d0_ref,
    d1_ref,
    d2_ref,
    d3_ref,
    p0_ref,
    p1_ref,
    p2_ref,
    p3_ref,
    q_ref,
    k_ref,
    v_ref,
    qraw_ref,
    kraw_ref,
    qgain_ref,
    kgain_ref,
    cos_ref,
    sin_ref,
    dqkv_ref,
    gains_ref,
    do_scr,
    dk_scr,
    dv_scr,
    head,
):
    z = at_ref[0]
    rows = d0_ref.shape[0]
    q_cols, k_cols = q_ref.shape[1], k_ref.shape[1]
    for r, d_ref in enumerate((d0_ref, d1_ref, d2_ref, d3_ref)):
        here = pl.ds(pl.multiple_of(lax.rem(z - r + SIDE, SIDE) * rows, rows), rows)
        do_scr[here] = d_ref[...]
    gains_ref[...] = jnp.zeros_like(gains_ref)
    for i in reversed(range(SIDE)):
        length = (i + 1) * rows
        here = slice(i * rows, (i + 1) * rows)
        kept_ref = (p0_ref, p1_ref, p2_ref, p3_ref)[i]
        d_queries = []
        for j in range(k_cols // head):
            k = k_ref[:length, j * head : (j + 1) * head]
            v = v_ref[:length, j * head : (j + 1) * head]
            d_key, d_value = 0.0, 0.0
            for h in (2 * j, 2 * j + 1):
                q = q_ref[here, h * head : (h + 1) * head]
                grad = do_scr[here, h * head : (h + 1) * head]
                probs_low = kept_ref[h]
                probs = probs_low.astype(F32)
                d_probs = nt(grad, v)
                inner = jnp.sum(probs * d_probs, axis=1, keepdims=True)
                d_scores = (probs * (d_probs - inner)).astype(BF)
                d_queries.append(nn(d_scores, k) * (head**-0.5))
                d_key = d_key + tn(d_scores, q)
                d_value = d_value + tn(probs_low, grad)
            if i == SIDE - 1:
                dk_scr[j] = d_key
                dv_scr[j] = d_value
            else:
                dk_scr[j, :length] += d_key
                dv_scr[j, :length] += d_value
        d_query = jnp.concatenate(d_queries, axis=1)
        d_query = turn(d_query, cos_ref[here], -sin_ref[here], head)
        d_raw, d_gain = norm_back(qraw_ref[here], d_query, qgain_ref[...], head)
        dqkv_ref[here, :q_cols] = d_raw.astype(BF)
        gains_ref[0:1] += d_gain
        d_key = jnp.concatenate([dk_scr[0, here], dk_scr[1, here]], axis=1)
        d_key = turn(d_key, cos_ref[here], -sin_ref[here], head)
        d_raw, d_gain = norm_back(kraw_ref[here], d_key, kgain_ref[...], head)
        dqkv_ref[here, q_cols : q_cols + k_cols] = d_raw.astype(BF)
        gains_ref[1:2, :k_cols] += d_gain
        d_value = jnp.concatenate([dv_scr[0, here], dv_scr[1, here]], axis=1)
        dqkv_ref[here, q_cols + k_cols :] = d_value.astype(BF)


def attend_back(at, d_rel, kept, q, k, v, q_raw, k_raw, qgain, kgain, cosine, sine):
    rows = d_rel[0].shape[0]
    length, q_cols = q.shape
    k_cols = k.shape[1]
    head = qgain.shape[0]

    def whole(shape):
        return pl.BlockSpec(shape, lambda g, at: (0,) * len(shape))

    def kernel(*refs):
        attend_back_kernel(*refs, head=head)

    operands = [
        *d_rel,
        *kept,
        q,
        k,
        v,
        q_raw,
        k_raw,
        jnp.tile(qgain, q_cols // head)[None],
        jnp.tile(kgain, k_cols // head)[None],
        cosine,
        sine,
    ]
    shapes = [((length, q_cols + 2 * k_cols), BF), ((8, q_cols), F32)]
    return pl.pallas_call(
        kernel,
        grid_spec=pltpu.PrefetchScalarGridSpec(
            num_scalar_prefetch=1,
            grid=(1,),
            in_specs=[whole(a.shape) for a in operands],
            out_specs=[whole(shape) for shape, _ in shapes],
            scratch_shapes=[
                pltpu.VMEM((length, q_cols), BF),
                pltpu.VMEM((k_cols // head, length, head), F32),
                pltpu.VMEM((k_cols // head, length, head), F32),
            ],
        ),
        out_shape=[jax.ShapeDtypeStruct(shape, dtype) for shape, dtype in shapes],
        compiler_params=pltpu.CompilerParams(vmem_limit_bytes=48 * MIB),
        cost_estimate=pl.CostEstimate(
            flops=8_000_000_000, bytes_accessed=8_000_000, transcendentals=4_000_000
        ),
        name="attend_back",
    )(at, *operands)


def expert_lines(routes, experts):
    line = lax.broadcasted_iota(jnp.int32, (experts, routes.shape[1]), 0).astype(F32)
    chosen = line == routes[0:1]
    for k in range(1, TOP):
        chosen = chosen | (line == routes[k : k + 1])
    return line, chosen


def pick_kernel(at_ref, cot_ref, down_ref, pick_ref, up_ref, dh_ref):
    tokens = pick_ref.shape[2]
    pick_iota = lax.broadcasted_iota(jnp.int32, (CAP, tokens), 0).astype(F32)
    tri = (
        lax.broadcasted_iota(jnp.int32, (tokens, tokens), 0)
        <= lax.broadcasted_iota(jnp.int32, (tokens, tokens), 1)
    ).astype(BF)
    mine = [at_ref[4 + j].astype(F32) for j in range(2)]
    members = []
    for s in range(SIDE):
        routes = cot_ref[0, s, tokens : tokens + 16, :tokens].astype(F32)
        for j in range(2):
            found = jnp.where(routes == mine[j], 1.0, 0.0)
            members.append(jnp.sum(found, axis=0, keepdims=True))
    member_all = jnp.concatenate(members, axis=0)
    rank_all = nn(member_all.astype(BF), tri)
    rank_all = jnp.where(member_all > 0.5, rank_all - 1.0, -1.0)
    for s in range(SIDE):
        for j in range(2):
            hit = pick_iota == rank_all[s * 2 + j : s * 2 + j + 1]
            pick_ref[s, j * CAP : (j + 1) * CAP] = jnp.where(hit, 1.0, 0.0).astype(BF)
        took = nn(pick_ref[s], cot_ref[0, s, :tokens]).astype(BF)
        for j in range(2):
            up_ref[j, s * CAP : (s + 1) * CAP] = took[j * CAP : (j + 1) * CAP]
    for j in range(2):
        dh_ref[j] = nt(up_ref[j], down_ref[j])


def moe_kernel(
    at_ref,
    rows_ref,
    routes_ref,
    pick_ref,
    dh_ref,
    router_ref,
    gate_ref,
    up_ref,
    back_a_ref,
    back_b_ref,
    x_ref,
    dgate_ref,
    dup_ref,
    hidden_ref,
    scaled_ref,
    share_ref,
    dgs_scr,
    b_scr,
):
    tokens = rows_ref.shape[2]
    half = rows_ref.shape[3] // 2
    y_here, chip = at_ref[2], at_ref[3]
    chip_row = lax.broadcasted_iota(jnp.int32, (SIDE * SIDE, half), 0) == chip
    mine = [at_ref[4 + j].astype(F32) for j in range(2)]
    for s in range(SIDE):
        rows = rows_ref[0, s]
        routes = routes_ref[0, s, :, :tokens].astype(F32)
        logits = nt(router_ref[...], rows)
        line, chosen = expert_lines(routes, router_ref.shape[0])
        top = jnp.max(jnp.where(chosen, logits, masked), axis=0, keepdims=True)
        expo = jnp.where(chosen, jnp.exp(jnp.minimum(logits - top, 0.0)), 0.0)
        share = expo / jnp.sum(expo, axis=0, keepdims=True)
        took = nn(pick_ref[s], rows).astype(BF)
        for j in range(2):
            own = jnp.sum(jnp.where(line == mine[j], share, 0.0), axis=0, keepdims=True)
            here = slice(s * CAP, (s + 1) * CAP)
            there = slice(j * CAP, (j + 1) * CAP)
            share_ref[j, here] = jnp.sum(
                pick_ref[s, there].astype(F32) * own, axis=1, keepdims=True
            )
            x_ref[j, here] = took[there]
    for j in range(2):
        x = x_ref[j]
        gate_act = nn(x, gate_ref[j])
        up_act = nn(x, up_ref[j])
        sig = 1.0 / (1.0 + jnp.exp(-gate_act))
        silu = gate_act * sig
        hidden = (silu * up_act).astype(BF)
        hidden_ref[j] = hidden
        scaled_ref[j] = (hidden.astype(F32) * share_ref[j]).astype(BF)
        raw = dh_ref[j]
        dgs_scr[j] = jnp.sum(hidden.astype(F32) * raw, axis=1, keepdims=True)
        d_hidden = raw * share_ref[j]
        d_gate = (d_hidden * up_act * (sig + silu * (1.0 - sig))).astype(BF)
        d_up = (d_hidden * silu).astype(BF)
        dgate_ref[j] = d_gate
        dup_ref[j] = d_up
        d_rows = (nt(d_gate, gate_ref[j]) + nt(d_up, up_ref[j])).astype(BF)
        for s in range(SIDE):
            b_scr[s, j * CAP : (j + 1) * CAP] = d_rows[s * CAP : (s + 1) * CAP]
    for s in range(SIDE):
        dy = lax.rem(s - y_here + SIDE, SIDE)
        back = tn(pick_ref[s], b_scr[s]).astype(BF)
        back_a_ref[0, dy, :tokens] = back[:, :half]
        back_b_ref[dy, 0, :tokens] = back[:, half:]
        found = []
        for j in range(2):
            col = dgs_scr[j, s * CAP : (s + 1) * CAP]
            pick = pick_ref[s, j * CAP : (j + 1) * CAP].astype(F32)
            found.append(jnp.sum(pick * col, axis=0, keepdims=True))
        found = jnp.where(chip_row, jnp.concatenate(found, axis=1), 0.0)
        high = found.astype(BF)
        back_a_ref[0, dy, tokens:] = high
        back_b_ref[dy, 0, tokens:] = (found - high.astype(F32)).astype(BF)


def result_kernel(at_ref, hidden_ref, share_ref, pick_ref, down_ref, out_ref, o_scr):
    for j in range(2):
        share = share_ref[j]
        result = nn(hidden_ref[j], down_ref[j]).astype(BF).astype(F32)
        gated = (share * result).astype(BF)
        for s in range(SIDE):
            o_scr[s, j * CAP : (j + 1) * CAP] = gated[s * CAP : (s + 1) * CAP]
    for s in range(SIDE):
        out_ref[0, s] = tn(pick_ref[s], o_scr[s]).astype(BF)


def over_sources(kernel, at, operands, outs, scratch, flops, name):
    return pl.pallas_call(
        kernel,
        grid_spec=pltpu.PrefetchScalarGridSpec(
            num_scalar_prefetch=1,
            grid=(SIDE,),
            in_specs=[pl.BlockSpec(block, index) for _, block, index in operands],
            out_specs=[pl.BlockSpec(block, index) for _, block, index in outs],
            scratch_shapes=scratch,
        ),
        out_shape=[jax.ShapeDtypeStruct(*what) for what, _, _ in outs],
        compiler_params=pltpu.CompilerParams(vmem_limit_bytes=60 * MIB),
        cost_estimate=pl.CostEstimate(flops=flops, bytes_accessed=30_000_000, transcendentals=0),
        name=name,
    )(at, *[array for array, _, _ in operands])


def source(g, at):
    return (at[1] + 2 + g) % SIDE


def by_source(rank, axis):
    return lambda g, at: tuple(source(g, at) if n == axis else 0 for n in range(rank))


def fixed(array):
    return array, array.shape, lambda g, at: (0,) * array.ndim


def moe_before(at, cot, down):
    _, _, padded, width = cot.shape
    tokens, slots, ff = padded - 16, SIDE * CAP, down.shape[1]
    return over_sources(
        pick_kernel,
        at,
        [(cot, (1, SIDE, padded, width), by_source(4, 0)), fixed(down)],
        [
            (((SIDE * SIDE, 2 * CAP, tokens), BF), (SIDE, 2 * CAP, tokens), by_source(3, 0)),
            (((2, SIDE * slots, width), BF), (2, slots, width), by_source(3, 1)),
            (((2, SIDE * slots, ff), F32), (2, slots, ff), by_source(3, 1)),
        ],
        [],
        4_000_000_000,
        "moe_before",
    )


def moe(at, rows, cot, pick, raw, router_t, gate, up):
    _, _, tokens, width = rows.shape
    padded = cot.shape[2]
    ff, slots, half = gate.shape[2], SIDE * CAP, width // 2

    def first(g, at):
        return ((2 + g) % SIDE, 0, 0, 0)

    def second(g, at):
        return (0, (2 + g) % SIDE, 0, 0)

    def kept(cols, dtype):
        return ((2, SIDE * slots, cols), dtype), (2, slots, cols), by_source(3, 1)

    return over_sources(
        moe_kernel,
        at,
        [
            (rows, (1, SIDE, tokens, width), by_source(4, 0)),
            (cot, (1, SIDE, 16, width), lambda g, at: (source(g, at), 0, tokens // 16, 0)),
            (pick, (SIDE, 2 * CAP, tokens), by_source(3, 0)),
            (raw, (2, slots, ff), by_source(3, 1)),
            fixed(router_t),
            fixed(gate),
            fixed(up),
        ],
        [
            (((SIDE, SIDE, padded, half), BF), (1, SIDE, padded, half), first),
            (((SIDE, SIDE, padded, half), BF), (SIDE, 1, padded, half), second),
            kept(width, BF),
            kept(ff, BF),
            kept(ff, BF),
            kept(ff, BF),
            kept(ff, BF),
            kept(1, F32),
        ],
        [pltpu.VMEM((2, slots, 1), F32), pltpu.VMEM((SIDE, 2 * CAP, width), BF)],
        14_000_000_000,
        "moe",
    )


def moe_result(at, hidden, share, pick, down):
    slots, ff, width = SIDE * CAP, hidden.shape[2], down.shape[2]
    tokens = pick.shape[2]

    def part(array):
        return array, (2, slots, array.shape[2]), by_source(3, 1)

    return over_sources(
        result_kernel,
        at,
        [part(hidden), part(share)]
        + [(pick, (SIDE, 2 * CAP, tokens), by_source(3, 0)), fixed(down)],
        [
            (((SIDE, SIDE, tokens, width), BF), (1, SIDE, tokens, width), by_source(4, 0)),
        ],
        [pltpu.VMEM((SIDE, 2 * CAP, width), BF)],
        4_000_000_000,
        "moe_result",
    )[0]


def middle_kernel(at_ref, a0_ref, a1_ref, a2_ref, a3_ref, x_ref, w_ref, gain_ref, mid_ref, low_ref):
    z = at_ref[0]
    cols = a0_ref.shape[1]
    total = x_ref[...].astype(F32)
    for r, a_ref in enumerate((a0_ref, a1_ref, a2_ref, a3_ref)):
        there = pl.ds(pl.multiple_of(lax.rem(z - r + SIDE, SIDE) * cols, cols), cols)
        total = total + nn(a_ref[...], w_ref[there])
    mid_ref[...] = total
    scale = lax.rsqrt(jnp.mean(total * total, axis=-1, keepdims=True) + epsilon)
    low_ref[...] = (total * scale * gain_ref[...]).astype(BF)


def in_vmem(kernel, at, operands, shapes, scratch, flops, name):
    def whole(shape):
        return pl.BlockSpec(shape, lambda g, at: (0,) * len(shape))

    return pl.pallas_call(
        kernel,
        grid_spec=pltpu.PrefetchScalarGridSpec(
            num_scalar_prefetch=1,
            grid=(1,),
            in_specs=[whole(a.shape) for a in operands],
            out_specs=[whole(shape) for shape, _ in shapes],
            scratch_shapes=scratch,
        ),
        out_shape=[jax.ShapeDtypeStruct(shape, dtype) for shape, dtype in shapes],
        compiler_params=pltpu.CompilerParams(vmem_limit_bytes=56 * MIB),
        cost_estimate=pl.CostEstimate(flops=flops, bytes_accessed=8_000_000, transcendentals=0),
        name=name,
    )(at, *operands)


def post_kernel(
    at_ref,
    a0_ref,
    a1_ref,
    a2_ref,
    b0_ref,
    b1_ref,
    b2_ref,
    mid_ref,
    low_ref,
    gain_ref,
    router_ref,
    routes_ref,
    cot_ref,
    w_ref,
    d_mid_ref,
    branch_ref,
    att0_ref,
    att1_ref,
    att2_ref,
    att3_ref,
    router_grad_ref,
    gain_grad_ref,
):
    z, core = at_ref[0], at_ref[6]
    tokens = mid_ref.shape[0]
    chips = SIDE * SIDE
    cols = att0_ref.shape[1]
    side_a = a0_ref[...].astype(F32) + a1_ref[...].astype(F32) + a2_ref[...].astype(F32)
    side_b = b0_ref[...].astype(F32) + b1_ref[...].astype(F32) + b2_ref[...].astype(F32)
    found = side_a[tokens:] + side_b[tokens:]
    d_gates = jnp.concatenate([found[:, :tokens], found[:, tokens:]], axis=0)
    line = lax.broadcasted_iota(jnp.int32, (2 * chips, tokens), 0)
    second = line >= chips
    expert = 2 * jnp.where(second, line - chips, line) + jnp.where(second, 1 - core, core)
    expert = expert.astype(F32)
    routes = routes_ref[...].astype(F32)
    chosen = expert == routes[0:1]
    for k in range(1, TOP):
        chosen = chosen | (expert == routes[k : k + 1])
    logits = nt(router_ref[...], low_ref[...])
    top = jnp.max(jnp.where(chosen, logits, masked), axis=0, keepdims=True)
    expo = jnp.where(chosen, jnp.exp(jnp.minimum(logits - top, 0.0)), 0.0)
    share = expo / jnp.sum(expo, axis=0, keepdims=True)
    d_gates = jnp.where(chosen, d_gates, 0.0)
    d_logits = share * (d_gates - jnp.sum(share * d_gates, axis=0, keepdims=True))
    d_logits = d_logits.astype(BF)
    router_grad_ref[...] = nn(d_logits, low_ref[...])
    d_normed = jnp.concatenate([side_a[:tokens], side_b[:tokens]], axis=1)
    d_normed = d_normed + tn(d_logits, router_ref[...])
    mid = mid_ref[...]
    scale = lax.rsqrt(jnp.mean(mid * mid, axis=-1, keepdims=True) + epsilon)
    gain_grad_ref[...] = jnp.sum(d_normed * mid * scale, axis=0, keepdims=True)
    weighted = d_normed * gain_ref[...]
    inner = jnp.mean(weighted * mid, axis=-1, keepdims=True)
    d_mid = cot_ref[...].astype(F32) + scale * weighted - mid * (scale * scale * scale) * inner
    d_mid_ref[...] = d_mid
    branch = d_mid.astype(BF)
    branch_ref[...] = branch
    for r, att_ref in enumerate((att0_ref, att1_ref, att2_ref, att3_ref)):
        there = pl.ds(pl.multiple_of(lax.rem(z + r, SIDE) * cols, cols), cols)
        att_ref[...] = nt(branch, w_ref[there]).astype(BF)


def weights_kernel(at_ref, normed_ref, dqkv_ref, att_ref, b0_ref, b1_ref, b2_ref, b3_ref, out_ref):
    cols = dqkv_ref.shape[1]
    rows, heads = att_ref.shape[1:]
    out_ref[:, :cols] = nn(normed_ref[...], dqkv_ref[...]).astype(BF)
    total = None
    for r, b_ref in enumerate((b0_ref, b1_ref, b2_ref, b3_ref)):
        part = tn(att_ref[(SIDE - r) % SIDE], b_ref[...])
        total = part if total is None else total + part
    total = total.astype(BF)
    for n in range(total.shape[1] // heads):
        out_ref[n * heads : (n + 1) * heads, cols:] = total[:, n * heads : (n + 1) * heads]


def finish_kernel(at_ref, *refs):
    pieces, (wq_ref, wk_ref, wv_ref, gain_ref) = refs[:16], refs[16:20]
    q_ref, k_ref, v_ref, o_ref, gain_grad_ref = refs[20:]
    z, x_at, y_at = at_ref[0], at_ref[1], at_ref[2]
    width = q_ref.shape[1]
    heads, kv = width // SIDE, k_ref.shape[1] // SIDE
    rows = width // (2 * SIDE * SIDE)

    def fill(refs_here):
        for side in range(2):
            for far in range(SIDE):
                ref = refs_here[side * SIDE + far]
                for near in range(SIDE):
                    rx, ry = (far, near) if side == 0 else (near, far)
                    xs, ys = lax.rem(x_at + rx, SIDE), lax.rem(y_at + ry, SIDE)
                    row = pl.multiple_of((xs * SIDE + ys) * rows, rows)
                    here = pl.ds(row, rows)
                    group = lax.div(row, heads)
                    inside = row - group * heads
                    at_o = pl.ds(pl.multiple_of(group * heads, heads), heads)
                    for rz in range(SIDE):
                        zs = lax.rem(z + rz, SIDE)
                        block = ref[near, rz].astype(F32)
                        at_q = pl.ds(pl.multiple_of(zs * heads, heads), heads)
                        at_k = pl.ds(pl.multiple_of(zs * kv, kv), kv)
                        if side == 0:
                            q_ref[here, at_q] = block[:, :heads]
                            k_ref[here, at_k] = block[:, heads:]
                        else:
                            v_ref[here, at_k] = block[:, :kv]
                            o_row = pl.multiple_of(zs * heads + inside, rows)
                            o_ref[pl.ds(o_row, rows), at_o] = block[:, kv:]

    @pl.when(pl.program_id(0) == 0)
    def _():
        fill(pieces[:8])

    @pl.when(pl.program_id(0) == 1)
    def _():
        fill(pieces[8:])

    for n in range(q_ref.shape[0] // heads):
        here = slice(n * heads, (n + 1) * heads)
        total = jnp.sum(q_ref[here] * wq_ref[here].astype(F32), axis=1, keepdims=True)
        total = total + jnp.sum(k_ref[here] * wk_ref[here].astype(F32), axis=1, keepdims=True)
        total = total + jnp.sum(v_ref[here] * wv_ref[here].astype(F32), axis=1, keepdims=True)
        total = jnp.broadcast_to(total, (heads, 128)).T[0:1]
        gain_grad_ref[:, here] = total / gain_ref[:, here]


def finish(at, ends, query_proj, key_proj, value_proj, gain):
    width = query_proj.shape[0]
    half = width // 2

    def which(g, at):
        return (at[6] + g) % 2

    def by_rows(cols):
        return pl.BlockSpec((half, cols), lambda g, at: (which(g, at), 0))

    def by_columns(rows):
        return pl.BlockSpec((rows, half), lambda g, at: (0, which(g, at)))

    kv = key_proj.shape[1]
    zeros = (0,) * ends[0].ndim
    return pl.pallas_call(
        finish_kernel,
        grid_spec=pltpu.PrefetchScalarGridSpec(
            num_scalar_prefetch=1,
            grid=(2,),
            in_specs=[pl.BlockSpec(end.shape, lambda g, at: zeros) for end in ends]
            + [by_rows(width), by_rows(kv), by_rows(kv), by_columns(1)],
            out_specs=[by_rows(width), by_rows(kv), by_rows(kv), by_columns(width), by_columns(1)],
        ),
        out_shape=[
            jax.ShapeDtypeStruct(shape, F32)
            for shape in ((width, width), (width, kv), (width, kv), (width, width), (1, width))
        ],
        compiler_params=pltpu.CompilerParams(vmem_limit_bytes=56 * MIB),
        cost_estimate=pl.CostEstimate(
            flops=10_000_000, bytes_accessed=24_000_000, transcendentals=0
        ),
        name="finish",
    )(at, *ends, query_proj, key_proj, value_proj, gain[None])


def rms_back(values, scale, gain, upstream):
    weighted = upstream * gain
    inner = jnp.mean(weighted * values, axis=-1, keepdims=True)
    return scale * weighted - values * (scale * scale * scale) * inner


def body(
    block_input,
    attn_norm_gain,
    query_proj,
    key_proj,
    value_proj,
    query_gain,
    key_gain,
    output_proj,
    ffn_norm_gain,
    router_proj,
    expert_routes,
    document_ids,
    expert_gate,
    expert_up,
    expert_down,
    cotangent,
):
    tokens, width = block_input.shape[1:]
    head = query_gain.shape[0]
    experts_all = router_proj.shape[1]
    z = lax.axis_index("dp")
    expert_at = lax.axis_index("expert")
    chip, core = expert_at // 2, expert_at % 2
    x_at, y_at = chip // SIDE, chip % SIDE
    at = jnp.stack([z, x_at, y_at, chip, expert_at, expert_at + 1 - 2 * core, core])
    at = at.astype(jnp.int32)

    own = block_input[0]
    route_rows = jnp.full((16, width), -1.0, BF)
    route_rows = lax.dynamic_update_slice(route_rows, expert_routes[0].T.astype(BF), (0, 0))
    cot_rows = jnp.concatenate([cotangent[0], route_rows], axis=0)
    own, cot_rows = tied(own, cot_rows)
    cot_all = lax.all_gather(cot_rows, "expert", axis_index_groups=plane_groups())
    x_rel = [own, along_z(own, 1), along_z(own, 2), along_z(own, -1)]

    doc = document_ids[0]
    below_one = jnp.sum((doc < 1).astype(jnp.int32))
    below_two = jnp.sum((doc < 2).astype(jnp.int32))
    start = jnp.where(doc < 1, 0, jnp.where(doc < 2, below_one, below_two)).astype(jnp.int32)
    position = (jnp.arange(doc.shape[0], dtype=jnp.int32) - start).astype(F32)
    frequency = theta ** (-jnp.arange(head // 2, dtype=F32) * 2.0 / head)
    angles = position[:, None] * frequency[None, :]
    cosine, sine = jnp.cos(angles), jnp.sin(angles)
    cosine = jnp.tile(cosine, (1, 4))
    sine = jnp.tile(jnp.concatenate([-sine, sine], axis=1), (1, 2))
    start = start[:, None]

    normed_all, q, k, v, q_raw, k_raw, out_rel, *kept_p = attend(
        at,
        x_rel,
        attn_norm_gain,
        query_proj,
        key_proj,
        value_proj,
        query_gain,
        key_gain,
        cosine,
        sine,
        start,
    )
    q_cols, k_cols = q.shape[1], k.shape[1]

    att_rel = [out_rel[0]] + [along_z(out_rel[r], t) for r, t in ((1, 1), (2, 2), (3, -1))]
    middle, normed_two = in_vmem(
        middle_kernel,
        at,
        [*att_rel, own, output_proj, ffn_norm_gain[None]],
        [((tokens, width), F32), ((tokens, width), BF)],
        [],
        600_000_000,
        "middle",
    )
    normed_two, cot_all = tied(normed_two, cot_all)
    rows_all = lax.all_gather(normed_two, "expert", axis_index_groups=plane_groups())
    gate_two = jnp.concatenate([expert_gate, swap_core(expert_gate)], axis=0)
    up_two = jnp.concatenate([expert_up, swap_core(expert_up)], axis=0)
    down_two = jnp.concatenate([expert_down, swap_core(expert_down)], axis=0)
    cot_all = cot_all.reshape(SIDE, SIDE, tokens + 16, width)
    pick, upstream, raw = moe_before(at, cot_all, down_two)
    back_a, back_b, kept_x, kept_dg, kept_du, kept_h, kept_s, share = moe(
        at,
        rows_all.reshape(SIDE, SIDE, tokens, width),
        cot_all,
        pick,
        raw,
        router_proj.T,
        gate_two,
        up_two,
    )
    out = moe_result(at, kept_h, share, pick, down_two)

    def slots_grad(a, b):
        return jnp.einsum("jrd,jrf->jdf", a, b, preferred_element_type=F32).astype(BF)

    first_a, first_b = ring_start(back_a, along_x), ring_start(back_b, along_y)
    gate_w = slots_grad(kept_x, kept_dg)
    up_a, down_a = ring_operands(back_a, first_a)
    up_b, down_b = ring_operands(back_b, first_b)
    up_a, down_a, up_b, down_b = tied(up_a, down_a, up_b, down_b)
    second_a = along_x(up_a, 1), along_x(down_a, -1)
    second_b = along_y(up_b, 1), along_y(down_b, -1)
    up_w = slots_grad(kept_x, kept_du)
    down_w = slots_grad(upstream, kept_s)
    second_a, second_b, gate_w, up_w, down_w, out = tied(
        second_a, second_b, gate_w, up_w, down_w, out
    )
    whole_w = jnp.stack([gate_w, up_w, down_w], axis=1)
    whole_w = (whole_w[0].astype(F32) + swap_core(whole_w[1]).astype(F32)).astype(BF)
    expert_sum = lax.psum_scatter(whole_w, "dp", scatter_dimension=1, tiled=True)
    part_a, part_b = low(ring_end(back_a, second_a)), low(ring_end(back_b, second_b))
    part_a, part_b = tied(part_a, part_b)
    first_a, first_b = ring_start(part_a, along_y), ring_start(part_b, along_x)
    up_a, down_a = ring_operands(part_a, first_a)
    up_b, down_b = ring_operands(part_b, first_b)
    up_a, down_a, up_b, down_b = tied(up_a, down_a, up_b, down_b)
    second_a = along_y(up_a, 1), along_y(down_a, -1)
    second_b = along_x(up_b, 1), along_x(down_b, -1)

    chips = SIDE * SIDE
    router_two = router_proj.T.reshape(chips, 2, width)
    router_two = jnp.where(core == 0, router_two, router_two[:, ::-1])
    router_two = router_two.transpose(1, 0, 2).reshape(experts_all, width)
    d_middle, d_branch, *d_att, router_local, ffn_gain_local = in_vmem(
        post_kernel,
        at,
        [part_a[0], *second_a, part_b[0], *second_b, middle, normed_two, ffn_norm_gain[None]]
        + [router_two, route_rows[:, :tokens], cotangent[0], output_proj],
        [
            ((tokens, width), F32),
            ((tokens, width), BF),
            *[((tokens, q_cols), BF)] * SIDE,
            ((experts_all, width), F32),
            ((1, width), F32),
        ],
        [],
        600_000_000,
        "post",
    )

    *d_att, out = tied(*d_att, out)
    d_rel = [d_att[0]] + [along_z(d_att[r], t) for r, t in ((1, 1), (2, 2), (3, -1))]
    out = lax.psum_scatter(
        out.reshape(chips * tokens, width),
        "expert",
        axis_index_groups=plane_groups(),
        scatter_dimension=0,
        tiled=True,
    )
    d_rel[1], d_branch_sent = tied(d_rel[1], d_branch)
    branch_rel = [d_branch] + [along_z(d_branch_sent, t) for t in (1, 2, -1)]
    router_local = jnp.where(core == 0, router_local, jnp.roll(router_local, chips, axis=0))
    few = jnp.concatenate([router_local, ffn_gain_local], axis=0)
    few = jnp.concatenate([few, jnp.zeros((15, width), F32)], axis=0).astype(BF)
    few, d_rel[2] = tied(few, d_rel[2])
    few = few.astype(F32) + sum(along_z(few, t).astype(F32) for t in (1, 2, -1))
    few = lax.dynamic_slice_in_dim(few[: experts_all + 1], z * q_cols, q_cols, axis=1)
    few = few.reshape(-1, 3 * q_cols)
    few = jnp.pad(few, ((0, 16 - few.shape[0]), (0, 0))).astype(BF)
    dqkv, gains = attend_back(
        at, d_rel, kept_p, q, k, v, q_raw, k_raw, query_gain, key_gain, cosine, sine
    )

    local = in_vmem(
        weights_kernel,
        at,
        [normed_all, dqkv, out_rel, *branch_rel],
        [((width, 2 * q_cols + 2 * k_cols), BF)],
        [],
        1_600_000_000,
        "weights",
    )[0]
    tail = jnp.concatenate([gains[0], gains[1], jnp.zeros_like(gains[0])])
    tail = jnp.pad(tail[None], ((0, 15), (0, 0))).astype(BF)
    tail = jnp.concatenate([tail, few], axis=0)
    half = width // 2
    mine = lax.dynamic_slice_in_dim(local, core * half, half, axis=0)
    other = lax.dynamic_slice_in_dim(local, (1 - core) * half, half, axis=0)
    got = swap_core(jnp.concatenate([other, tail], axis=0)).astype(F32)
    part = (mine.astype(F32) + got[:half]).astype(BF)
    tail = (tail.astype(F32) + got[half:]).astype(BF)
    part, tail = scatter_sum(part, tail, x_at, along_x)
    part, tail = scatter_sum(part, tail, y_at, along_y)
    pieces = jnp.stack(ring_pieces(jnp.concatenate([part, tail], axis=0), along_z))
    rows = part.shape[0]
    gain_sums = jnp.sum(pieces[:, rows].astype(F32), axis=0)
    few = pieces[:, rows + 16 : rows + 16 + (experts_all + 1) * q_cols // (3 * q_cols)]
    few = few.astype(F32).reshape(SIDE, experts_all + 1, q_cols)
    few = jnp.roll(few, z, axis=0).transpose(1, 0, 2).reshape(experts_all + 1, width)
    router_sum = few[:experts_all].reshape(2, chips, width).transpose(2, 1, 0)
    router_sum = router_sum.reshape(width, experts_all)
    split = q_cols + k_cols
    side_a, side_b = pieces[:, :rows, :split], pieces[:, :rows, split:]
    side_a = jnp.stack(ring_pieces(side_a, along_y))
    side_b = jnp.stack(ring_pieces(side_b, along_x))
    ends = ring_pieces(side_a, along_x) + ring_pieces(side_b, along_y)
    ends = ends + [swap_core(piece) for piece in ends]
    query_sum, key_sum, value_sum, output_sum, attn_gain_sum = finish(
        at, ends, query_proj, key_proj, value_proj, attn_norm_gain
    )
    query_gain_sum = jnp.sum(gain_sums[:q_cols].reshape(-1, head), axis=0)
    key_gain_sum = jnp.sum(gain_sums[q_cols : q_cols + k_cols].reshape(-1, head), axis=0)

    expert_sum = expert_sum.astype(F32)
    gate_grad, up_grad = expert_sum[0:1], expert_sum[1:2]
    down_grad = jnp.transpose(expert_sum[2:3], (0, 2, 1))

    back = jnp.zeros((tokens, SIDE, q_cols + 2 * k_cols), BF)
    for r, step in ((0, 0), (1, 1), (2, 2), (3, -1)):
        piece = block_at(dqkv, z + r, tokens)
        piece = along_z(piece, step) if step else piece
        back = lax.dynamic_update_slice(back, piece[:, None], (0, (z - r) % SIDE, 0))
    d_query = back[:, :, :q_cols].reshape(tokens, -1)
    d_key = back[:, :, q_cols : q_cols + k_cols].reshape(tokens, -1)
    d_value = back[:, :, q_cols + k_cols :].reshape(tokens, -1)
    d_normed = nt(d_query, query_proj) + nt(d_key, key_proj) + nt(d_value, value_proj)
    inputs = own.astype(F32)
    scale_one = lax.rsqrt(jnp.mean(inputs * inputs, axis=-1, keepdims=True) + epsilon)
    input_grad = d_middle + rms_back(inputs, scale_one, attn_norm_gain, d_normed)

    block_output = (middle + out.astype(F32)).astype(BF)

    return (
        block_output[None],
        input_grad[None],
        attn_gain_sum[0],
        query_sum,
        key_sum,
        value_sum,
        query_gain_sum,
        key_gain_sum,
        output_sum,
        few[experts_all],
        router_sum,
        gate_grad,
        up_grad,
        down_grad,
    )


def solution(mesh):
    tokens = P("expert", "dp", None)
    experts = P("expert", None, None)
    return jax.shard_map(
        body,
        mesh=mesh,
        in_specs=(tokens,)
        + (P(),) * 9
        + (tokens, P("expert", None), experts, experts, experts, tokens),
        out_specs=(tokens, tokens)
        + (P(),) * 9
        + (tokens, tokens, P("expert", None, "dp")),
        check_vma=False,
    )
```
